128 devices in a mesh: fsdp: 32 (over x, y, core), ctx: 4 (over z).
Axes of the slice: x: 4, y: 4, z: 4, core: 2. Of those that a mesh axis runs over, the one named last changes fastest.
Arguments:
- tokens: bfloat16 [64, 512, 768], P('fsdp', 'ctx'), may hold values from -6 to 6
- cotangent: bfloat16 [64, 512, 768], P('fsdp', 'ctx'), may hold values from -6 to 6
- lengths: int32 [64, 4], P('fsdp'), may hold values from 0 to 512, as said below
- input_weight: float32 [768, 2304], P('fsdp'), may hold values from -0.21875 to 0.21875
- output_weight: float32 [768, 768], P('fsdp'), may hold values from -0.4375 to 0.4375
- expand_weight: float32 [768, 3072], P('fsdp'), may hold values from -0.21875 to 0.21875
- shrink_weight: float32 [3072, 768], P('fsdp'), may hold values from -0.109375 to 0.109375
- vectors: float32 [768, 8], P('fsdp'), may hold values from -1.2 to 1.3
- expand_bias: float32 [3072], P('fsdp'), may hold values from -1.2 to 1.2
- input_moment: float32 [768, 2304], P('fsdp'), may hold values from -40.18629 to 40.18629
- output_moment: float32 [768, 768], P('fsdp'), may hold values from -40.18629 to 40.18629
- expand_moment: float32 [768, 3072], P('fsdp'), may hold values from -40.18629 to 40.18629
- shrink_moment: float32 [3072, 768], P('fsdp'), may hold values from -40.18629 to 40.18629
- vectors_moment: float32 [768, 8], P('fsdp'), may hold values from -80.372585 to 80.372585
- biases_moment: float32 [3072], P('fsdp'), may hold values from -40.18629 to 40.18629
- input_square: float32 [768, 2304], P('fsdp'), may hold values from 8.192 to 32.768
- output_square: float32 [768, 768], P('fsdp'), may hold values from 8.192 to 32.768
- expand_square: float32 [768, 3072], P('fsdp'), may hold values from 8.192 to 32.768
- shrink_square: float32 [3072, 768], P('fsdp'), may hold values from 8.192 to 32.768
- vectors_square: float32 [768, 8], P('fsdp'), may hold values from 32.768 to 131.072
- biases_square: float32 [3072], P('fsdp'), may hold values from 8.192 to 32.768
Outputs:
- layer_output: bfloat16 [64, 512, 768], P('fsdp', 'ctx')
- tokens_gradient: float32 [64, 512, 768], P('fsdp', 'ctx')
- updated_input: float32 [768, 2304], P('fsdp')
- updated_output: float32 [768, 768], P('fsdp')
- updated_expand: float32 [768, 3072], P('fsdp')
- updated_shrink: float32 [3072, 768], P('fsdp')
- updated_vectors: float32 [768, 8], P('fsdp')
- updated_biases: float32 [3072], P('fsdp')
- average_input: float32 [768, 2304], P('fsdp')
- average_output: float32 [768, 768], P('fsdp')
- average_expand: float32 [768, 3072], P('fsdp')
- average_shrink: float32 [3072, 768], P('fsdp')
- average_vectors: float32 [768, 8], P('fsdp')
- average_biases: float32 [3072], P('fsdp')
- squares_input: float32 [768, 2304], P('fsdp')
- squares_output: float32 [768, 768], P('fsdp')
- squares_expand: float32 [768, 3072], P('fsdp')
- squares_shrink: float32 [3072, 768], P('fsdp')
- squares_vectors: float32 [768, 8], P('fsdp')
- squares_biases: float32 [3072], P('fsdp')
The draws below stay inside these ranges and needn't reach their ends.
Inputs may be any that keep to these rules, and one draw needn't show every extreme that they name: Row g holds the lengths of the sequences packed in that order from position 0 of pack g; the positions after them up to 512 are padding, a multiple of 128 and fewer than 128; some sequence of every row starts within the first 128 positions and ends within the last 128; some row is a single sequence of 512.
All inputs are finite; a program needn't handle non-finite values.
Results may differ from the reference program's by a relative error of at most 0.025.
Values may be sent and summed in bfloat16 or wider, within the bound.
A program may use at most 128 MiB of HBM per device.

```python
import math
import jax
import jax.numpy as jnp
from jax import lax

D = 768
H = 12
HD = 64
FF = 3072
TOK_DEV = 128
SEQS = 4
BLOCK = 128
STEP = 10
LEN = 512
GROUPS = 64
TOKENS = 32768


def first_moment(key, shape, typical):
    noise = jnp.clip(jax.random.normal(key, shape, jnp.float32), -4.0, 4.0)
    return 0.111 * typical * noise


def draw_lengths(key, part):
    key = jax.random.fold_in(key, 7)
    keys = jax.random.split(key, 5)
    chosen = jax.random.randint(keys[0], (), 0, GROUPS)
    rows = jnp.arange(GROUPS, dtype=jnp.int32)
    padding = jax.random.randint(keys[1], (GROUPS,), 0, TOK_DEV // BLOCK) * BLOCK
    padding = jnp.where(rows == chosen, 0, padding)
    room = TOK_DEV - padding
    others = jax.random.randint(keys[2], (GROUPS,), 0, room)
    others = jnp.where(rows == chosen, 0, others)
    cuts = jax.random.randint(keys[3], (GROUPS, SEQS - 2), 0, others[:, None] + 1)
    cuts = jnp.sort(cuts, axis=1)
    edges = jnp.concatenate([jnp.zeros((GROUPS, 1), jnp.int32), cuts, others[:, None]], axis=1)
    shorts = edges[:, 1:] - edges[:, :-1]
    longest = LEN - padding - others
    slot = jax.random.randint(keys[4], (GROUPS,), 0, SEQS)
    columns = []
    for index in range(SEQS):
        before = shorts[:, index] if index < SEQS - 1 else shorts[:, 0]
        after = shorts[:, index - 1] if index > 0 else shorts[:, 0]
        picked = jnp.where(index < slot, before, jnp.where(index == slot, longest, after))
        columns.append(picked)
    return jnp.stack(columns, axis=1).astype(jnp.int32)


def draw_vectors(key, part):
    key = jax.random.fold_in(key, 11)
    first_key, second_key = jax.random.split(key)
    gains = 1.0 + 0.3 * jax.random.uniform(first_key, (D, 8), jnp.float32, -1.0, 1.0)
    shifts = 0.3 * jnp.clip(jax.random.normal(second_key, (D, 8), jnp.float32), -4.0, 4.0)
    column = jnp.arange(8, dtype=jnp.int32)
    return jnp.where((column == 0) | (column == 5), gains, shifts)


def draw_input_moment(key, part):
    key = jax.random.fold_in(key, 21)
    return first_moment(key, (D, 3 * D), 0.5 * math.sqrt(TOKENS))


def draw_output_moment(key, part):
    key = jax.random.fold_in(key, 22)
    return first_moment(key, (D, D), 0.5 * math.sqrt(TOKENS))


def draw_expand_moment(key, part):
    key = jax.random.fold_in(key, 23)
    return first_moment(key, (D, FF), 0.5 * math.sqrt(TOKENS))


def draw_shrink_moment(key, part):
    key = jax.random.fold_in(key, 24)
    return first_moment(key, (FF, D), 0.5 * math.sqrt(TOKENS))


def draw_vectors_moment(key, part):
    key = jax.random.fold_in(key, 25)
    return first_moment(key, (D, 8), math.sqrt(TOKENS))


def draw_biases_moment(key, part):
    key = jax.random.fold_in(key, 26)
    return first_moment(key, (FF,), 0.5 * math.sqrt(TOKENS))


def block_levels(stream_key, shape, pieces, least, high):
    def one(position, blocks):
        draws = jax.random.uniform(jax.random.fold_in(jax.random.fold_in(stream_key, 6), position), (blocks,), jnp.float32, least / len(pieces), high / len(pieces))
        return jnp.repeat(jnp.exp(draws), shape[position] // blocks).reshape((-1,) + (1,) * (len(shape) - position - 1))

    level = one(*pieces[0])
    for cut in pieces[1:]:
        level = level * one(*cut)
    return level


def centred(rng, dims, scale, bound, cuts=(), held_as=jnp.bfloat16):
    level = block_levels(rng, dims, cuts, -0.22, 0.18) if cuts else 1.0
    drawn = jax.random.normal(rng, dims, jnp.float32) * scale * level
    return jnp.minimum(jnp.maximum(drawn, -bound), bound).astype(held_as)


def setup_inputs(seed: int = 0) -> dict:
    key_list = jax.random.split(jax.random.key(seed), 22)
    return {
        "tokens": centred(key_list[0], (GROUPS, LEN, D), 1.0, 6.0, ((0, 32), (1, 4))),
        "cotangent": centred(key_list[1], (GROUPS, LEN, D), 1.0, 6.0, ((0, 32), (1, 4))),
        "lengths": draw_lengths(jax.random.fold_in(key_list[21], 71), 0),
        "input_weight": centred(key_list[3], (D, 3 * D), D ** -0.5, 0.21875, ((0, 32),), jnp.float32),
        "output_weight": centred(key_list[4], (D, D), (D // 4) ** -0.5, 0.4375, ((0, 32),), jnp.float32),
        "expand_weight": centred(key_list[5], (D, FF), D ** -0.5, 0.21875, ((0, 32),), jnp.float32),
        "shrink_weight": centred(key_list[6], (FF, D), FF ** -0.5, 0.109375, ((0, 32),), jnp.float32),
        "vectors": draw_vectors(jax.random.fold_in(key_list[21], 71), 0),
        "expand_bias": centred(key_list[8], (FF,), 0.3, 1.2, ((0, 32),), jnp.float32),
        "input_moment": draw_input_moment(jax.random.fold_in(key_list[21], 71), 0),
        "output_moment": draw_output_moment(jax.random.fold_in(key_list[21], 71), 0),
        "expand_moment": draw_expand_moment(jax.random.fold_in(key_list[21], 71), 0),
        "shrink_moment": draw_shrink_moment(jax.random.fold_in(key_list[21], 71), 0),
        "vectors_moment": draw_vectors_moment(jax.random.fold_in(key_list[21], 71), 0),
        "biases_moment": draw_biases_moment(jax.random.fold_in(key_list[21], 71), 0),
        "input_square": jnp.clip(jnp.exp(math.log(32.768) - 1.3862944 * jax.random.uniform(key_list[15], (D, 3 * D), jnp.float32) ** block_levels(key_list[15], (D, 3 * D), ((0, 32),), -0.2, 0.2)), 8.192, 32.768),
        "output_square": jnp.clip(jnp.exp(math.log(32.768) - 1.3862944 * jax.random.uniform(key_list[16], (D, D), jnp.float32) ** block_levels(key_list[16], (D, D), ((0, 32),), -0.2, 0.2)), 8.192, 32.768),
        "expand_square": jnp.clip(jnp.exp(math.log(32.768) - 1.3862944 * jax.random.uniform(key_list[17], (D, FF), jnp.float32) ** block_levels(key_list[17], (D, FF), ((0, 32),), -0.2, 0.2)), 8.192, 32.768),
        "shrink_square": jnp.clip(jnp.exp(math.log(32.768) - 1.3862944 * jax.random.uniform(key_list[18], (FF, D), jnp.float32) ** block_levels(key_list[18], (FF, D), ((0, 32),), -0.2, 0.2)), 8.192, 32.768),
        "vectors_square": jnp.clip(jnp.exp(math.log(131.072) - 1.3862944 * jax.random.uniform(key_list[19], (D, 8), jnp.float32) ** block_levels(key_list[19], (D, 8), ((0, 32),), -0.2, 0.2)), 32.768, 131.072),
        "biases_square": jnp.clip(jnp.exp(math.log(32.768) - 1.3862944 * jax.random.uniform(key_list[20], (FF,), jnp.float32) ** block_levels(key_list[20], (FF,), ((0, 32),), -0.2, 0.2)), 8.192, 32.768),
    }


norm_eps = 1e-05
beta_first = 0.9
beta_second = 0.999
adam_eps = 1e-08
decay_rate = 0.01
highest = lax.Precision.HIGHEST

@jax.custom_vjp
def low(v):
    return lax.optimization_barrier(v.astype(jnp.bfloat16)).astype(jnp.float32)

@jax.custom_vjp
def low_back(v):
    return v

def low_keep(v):
    return (low(v), None)

def low_pass(kept, grad):
    return (grad,)

def back_keep(v):
    return (v, None)

def back_low(kept, grad):
    return (low(grad),)
low.defvjp(low_keep, low_pass)
low_back.defvjp(back_keep, back_low)

def normalize(values, gain, shift):
    center = values - lax.optimization_barrier(jnp.mean(values, -1, keepdims=True))
    scale_inv = lax.rsqrt(lax.optimization_barrier(jnp.mean(center * center, -1, keepdims=True)) + norm_eps)
    return center * scale_inv * gain + shift

def attention(query, keys, values, segment):
    total = query.shape[0]
    rows = min(512, total)
    heads_query = query.reshape(total, H, HD)
    heads_keys = keys.reshape(total, H, HD)
    heads_values = values.reshape(total, H, HD)
    scale = HD ** (-0.5)
    col_pos = jnp.arange(total, dtype=jnp.int32)

    def block(start):
        query_block = lax.dynamic_slice_in_dim(heads_query, start, rows, 0)
        row_seg = lax.dynamic_slice_in_dim(segment, start, rows, 0)
        row_pos = start + jnp.arange(rows, dtype=jnp.int32)
        scores = jnp.einsum('qhd,khd->hqk', query_block, heads_keys, precision=highest, preferred_element_type=jnp.float32) * scale
        scores = low_back(scores)
        allowed = (row_seg[:, None] == segment[None, :]) & (col_pos[None, :] <= row_pos[:, None])
        scores = jnp.where(allowed[None], scores, -1e+30)
        peak = lax.optimization_barrier(jnp.max(scores, -1, keepdims=True))
        raised = jnp.exp(scores - peak)
        probs = low(raised / lax.optimization_barrier(jnp.sum(raised, -1, keepdims=True)))
        return jnp.einsum('hqk,khd->qhd', probs, heads_values, precision=highest, preferred_element_type=jnp.float32)
    starts = jnp.arange(total // rows, dtype=jnp.int32) * rows
    blocks = lax.map(jax.checkpoint(block), starts)
    return blocks.reshape(total, H * HD)

def matmul(left, right):
    return jnp.dot(left, right, precision=highest, preferred_element_type=jnp.float32)

def forward(tokens, input_weight, output_weight, expand_weight, shrink_weight, vectors, expand_bias, segment, live):
    input_weight = low(input_weight)
    output_weight = low(output_weight)
    expand_weight = low(expand_weight)
    shrink_weight = low(shrink_weight)
    vectors = low(vectors)
    expand_bias = low(expand_bias)
    normed = low(normalize(tokens, vectors[:, 0], vectors[:, 1]))
    projected = matmul(normed, input_weight)
    query = low_back(low(projected[:, :D] + vectors[:, 2]))
    keys = low_back(low(projected[:, D:2 * D]))
    values = low_back(low(projected[:, 2 * D:] + vectors[:, 3]))
    context = low_back(low(attention(query, keys, values, segment)))
    after_attn = tokens + low_back(matmul(context, output_weight) + vectors[:, 4])
    second = low(normalize(after_attn, vectors[:, 5], vectors[:, 6]))
    expanded = low_back(matmul(second, expand_weight) + expand_bias)
    hidden = low(jax.nn.gelu(expanded, approximate=False))
    result = after_attn + matmul(hidden, shrink_weight) + vectors[:, 7]
    return result * live[:, None]

def adam_step(weight, gradient, moment, square, rate):
    moment_new = beta_first * moment + (1.0 - beta_first) * gradient
    square_new = beta_second * square + (1.0 - beta_second) * gradient * gradient
    corrected = moment_new / (1.0 - beta_first ** STEP)
    spread = jnp.sqrt(square_new / (1.0 - beta_second ** STEP)) + adam_eps
    return (weight - rate * (corrected / spread + decay_rate * weight), moment_new, square_new)

def reference(tokens, cotangent, lengths, input_weight, output_weight, expand_weight, shrink_weight, vectors, expand_bias, input_moment, output_moment, expand_moment, shrink_moment, vectors_moment, biases_moment, input_square, output_square, expand_square, shrink_square, vectors_square, biases_square):
    ends = jnp.cumsum(lengths, axis=1, dtype=jnp.int32)
    positions = jnp.arange(LEN, dtype=jnp.int32)
    segment = lax.optimization_barrier(jnp.sum((positions[None, :, None] >= ends[:, None, :]).astype(jnp.int32), axis=2, dtype=jnp.int32))
    live = (segment < SEQS).astype(jnp.float32)
    params = (input_weight, output_weight, expand_weight, shrink_weight, vectors, expand_bias)
    packs = tokens.astype(jnp.float32)
    backs = cotangent.astype(jnp.float32)

    def one_pack(totals, inputs):
        pack, back, seg_pack, live_pack = inputs

        def apply(pack_in, *weights):
            return forward(pack_in, *weights, seg_pack, live_pack)
        result, pull = jax.vjp(apply, pack, *params)
        grads = pull(back)
        summed = tuple((total_part + grad_part for total_part, grad_part in zip(totals, grads[1:])))
        return (summed, (result, grads[0]))
    start_totals = tuple((jnp.zeros_like(weight) for weight in params))
    totals, outputs = lax.scan(one_pack, start_totals, (packs, backs, segment, live))
    layer_output = outputs[0].astype(jnp.bfloat16)
    tokens_gradient = outputs[1]
    moments = (input_moment, output_moment, expand_moment, shrink_moment, vectors_moment, biases_moment)
    squares = (input_square, output_square, expand_square, shrink_square, vectors_square, biases_square)
    rates = (2.0 * D ** (-0.5), 4.0 * D ** (-0.5), 2.0 * D ** (-0.5), 2.0 * FF ** (-0.5), 1.0, 1.0)
    new_input = adam_step(params[0], totals[0], moments[0], squares[0], rates[0])
    new_output = adam_step(params[1], totals[1], moments[1], squares[1], rates[1])
    new_expand = adam_step(params[2], totals[2], moments[2], squares[2], rates[2])
    new_shrink = adam_step(params[3], totals[3], moments[3], squares[3], rates[3])
    new_vectors = adam_step(params[4], totals[4], moments[4], squares[4], rates[4])
    new_biases = adam_step(params[5], totals[5], moments[5], squares[5], rates[5])
    return (layer_output, tokens_gradient, new_input[0], new_output[0], new_expand[0], new_shrink[0], new_vectors[0], new_biases[0], new_input[1], new_output[1], new_expand[1], new_shrink[1], new_vectors[1], new_biases[1], new_input[2], new_output[2], new_expand[2], new_shrink[2], new_vectors[2], new_biases[2])
```

```python
import jax, jax.numpy as jnp
from jax import lax
from jax.experimental import pallas as pl
from jax.experimental.pallas import tpu as pltpu
from jax.sharding import PartitionSpec as P

MESH = pl.DeviceIdType.MESH
BF = jnp.bfloat16
F32 = jnp.float32


def flip1(v):
    return v + 1 - 2 * (v % 2)


class Links:
    def __init__(self, send_sems, recv_sems):
        self.send_sems, self.recv_sems, self.used = send_sems, recv_sems, 0
        me = lax.axis_index("fsdp")
        self.z = lax.axis_index("ctx")
        self.core = me % 2
        self.chip = me // 2
        self.x, self.y = self.chip // 4, self.chip % 4
        self.sib = {"fsdp": me + 1 - 2 * self.core}
        self.pending = []

    def at(self, axis, kind):
        v = {"x": self.x, "y": self.y, "z": self.z}[axis]
        return flip1(v) if kind == 1 else 3 - v

    def dev(self, axis, kind):
        if axis == "z":
            return {"ctx": self.at("z", kind)}
        x = self.at("x", kind) if axis == "x" else self.x
        y = self.at("y", kind) if axis == "y" else self.y
        return {"fsdp": (x * 4 + y) * 2 + self.core}

    def send(self, src, dst, device):
        i = self.used
        self.used += 1
        copy = pltpu.make_async_remote_copy(
            src_ref=src, dst_ref=dst, send_sem=self.send_sems.at[i],
            recv_sem=self.recv_sems.at[i], device_id=device, device_id_type=MESH,
        )
        copy.start()
        self.pending.append(copy)
        return copy

    def barrier(self, devices):
        sem = pltpu.get_barrier_semaphore()
        for d in devices:
            pl.semaphore_signal(sem, inc=1, device_id=d, device_id_type=MESH)
        pl.semaphore_wait(sem, len(devices))

    def sent(self, copy):
        copy.wait_send()
        self.pending = [q for q in self.pending if q is not copy]

    def drain(self):
        for c in self.pending:
            c.wait_send()
        self.pending = []


ORDERS = (
    (("y", 1), ("y", 3), ("x", 1), ("x", 3)),
    (("y", 3), ("y", 1), ("x", 3), ("x", 1)),
    (("x", 1), ("x", 3), ("y", 1), ("y", 3)),
    (("x", 3), ("x", 1), ("y", 3), ("y", 1)),
)


def held(v, kind, count):
    if count == 0:
        return [(v, 1)]
    if count == 2:
        return [(0, 4)]
    if kind == 1:
        return [(v - v % 2, 2)]
    return [(v, 1), (3 - v, 1)]


def regions(links, flavor, step, coords):
    order = ORDERS[flavor]
    first, second = order[0][0], order[2][0]
    a = held(coords[first], order[0][1], min(step, 2))
    b = held(coords[second], order[2][1], max(step - 2, 0))
    out = []
    for i, (sa, na) in enumerate(a):
        for j, (sb, nb) in enumerate(b):
            sel = {first: pl.ds(sa, na), second: pl.ds(sb, nb)}
            out.append((sel["x"], sel["y"], i, j, {first: na, second: nb}))
    return out


def gather_step(links, pieces, step):
    copies = []
    for flavor, view in pieces:
        axis, kind = ORDERS[flavor][step]
        device = links.dev(axis, kind)
        for xs, ys, *_ in regions(links, flavor, step, {"x": links.x, "y": links.y}):
            copies.append(links.send(view(xs, ys), view(xs, ys), device))
    return copies


def pair_of(v, kind):
    if kind == 1:
        return [v - v % 2, v - v % 2 + 1]
    return [v, 3 - v]


class Scatter:
    def __init__(self, links, pieces, bufs):
        self.links, self.pieces, self.bufs = links, pieces, bufs

    def _sel(self, flavor, a, b):
        first = ORDERS[flavor][0][0]
        return (a, b) if first == "x" else (b, a)

    def start(self, step):
        L = self.links
        self.copies = []
        for flavor, acc, sub in self.pieces:
            order = ORDERS[flavor]
            axis, kind = order[3 - step]
            first, second = order[0][0], order[2][0]
            va, vb = {"x": L.x, "y": L.y}[first], {"x": L.x, "y": L.y}[second]
            p = L.at(axis, kind)
            dev = L.dev(axis, kind)
            if step == 0:
                for j, b in enumerate(pair_of(p, order[2][1])):
                    self.copies.append(L.send(acc(*self._sel(flavor, pl.ds(0, 4), b)), sub(self.bufs[0].at[j]), dev))
            elif step == 1:
                self.copies.append(L.send(acc(*self._sel(flavor, pl.ds(0, 4), p)), sub(self.bufs[1]), dev))
            elif step == 2:
                for j, a in enumerate(pair_of(p, order[0][1])):
                    self.copies.append(L.send(acc(*self._sel(flavor, a, vb)), sub(self.bufs[2].at[j]), dev))
            else:
                self.copies.append(L.send(acc(*self._sel(flavor, p, vb)), sub(self.bufs[3]), dev))

    def finish(self, step):
        L = self.links
        for c in self.copies:
            c.wait_recv()

        def add(view, buf):
            view[...] = (view[...].astype(F32) + buf[...].astype(F32)).astype(BF)

        for flavor, acc, sub in self.pieces:
            order = ORDERS[flavor]
            first, second = order[0][0], order[2][0]
            va, vb = {"x": L.x, "y": L.y}[first], {"x": L.x, "y": L.y}[second]
            if step == 0:
                for j, b in enumerate(pair_of(vb, order[2][1])):
                    for a in range(4):
                        add(acc(*self._sel(flavor, a, b)), sub(self.bufs[0].at[j, a]))
            elif step == 1:
                for a in range(4):
                    add(acc(*self._sel(flavor, a, vb)), sub(self.bufs[1].at[a]))
            elif step == 2:
                for j, a in enumerate(pair_of(va, order[0][1])):
                    add(acc(*self._sel(flavor, a, vb)), sub(self.bufs[2].at[j]))
            else:
                add(acc(*self._sel(flavor, va, vb)), sub(self.bufs[3]))


def lanes(n, size):
    return lambda ref: ref.at[..., pl.ds(n, size)]


def rows(n, size):
    return lambda ref: ref.at[..., pl.ds(n, size), :]


PIECES = (
    tuple((f, lanes(f * 128, 128)) for f in range(3)) + ((3, lanes(384, 384)),),
    tuple((f, lanes(f * 384, 384)) for f in range(4)),
    tuple((f, rows(f * 48, 48)) for f in range(4)),
)


D = 768
H = 12
HD = 64
FF = 3072
STEP = 10


norm_eps = 1e-05
beta_first = 0.9
beta_second = 0.999
adam_eps = 1e-08
decay_rate = 0.01


def normalize(values, gain, shift):
    center = values - jnp.mean(values, -1, keepdims=True)
    scale_inv = lax.rsqrt(jnp.mean(center * center, -1, keepdims=True) + norm_eps)
    return center * scale_inv * gain + shift


def adam_step(weight, gradient, moment, square, rate):
    moment_new = beta_first * moment + (1.0 - beta_first) * gradient
    square_new = beta_second * square + (1.0 - beta_second) * gradient * gradient
    corrected = moment_new / (1.0 - beta_first**STEP)
    spread = jnp.sqrt(square_new / (1.0 - beta_second**STEP)) + adam_eps
    return (weight - rate * (corrected / spread + decay_rate * weight), moment_new, square_new)


def gather_kernel(win, wout, wexp, wshr, tok, sm, G0, G1, G2, X, SM, sbuf, f0a, f0b, f1, f2, ss, rs, ls):
    L=Links(ss, rs)
    c, chip = L.core, L.chip
    devs=[L.sib]+[L.dev(a,k) for a in "xyz" for k in (1,3)]
    L.barrier(devs)
    small=[]
    stages=[L.sib]+[L.dev(a,k) for a,k in (("y",1),("y",3),("x",1),("x",3))]
    def small_start(i): small.append(L.send(sbuf.at[0], sbuf.at[i+1], stages[i]))
    def small_finish(i):
        small[i].wait_recv(); L.sent(small[i])
        sbuf[0]=sbuf[0]+sbuf[i+1]
    sbuf[0]=sm[...]
    small_start(0)
    row = pl.multiple_of(24*c, 8)
    row96 = pl.multiple_of(96*c, 8)
    def halves(src, n, dst, r, nr):
        other = pl.multiple_of((1-c)*n, 128); mine = pl.multiple_of(c*n,128)
        cp = L.send(src.at[:, pl.ds(other,n)], dst.at[pl.ds(r,nr)], L.sib)
        i = halves.n; halves.n += 1
        lc = pltpu.make_async_copy(src.at[:, pl.ds(mine,n)], dst.at[pl.ds(r,nr)], ls.at[i]); lc.start()
        return cp, lc
    halves.n=0
    s0=[halves(win,384,f0a,row,24), halves(wout,384,f0b,row,24), halves(wexp,1536,f1,row,24), halves(wshr,384,f2,row96,96)]
    lt = pltpu.make_async_copy(tok, X.at[:, L.z], ls.at[4]); lt.start();
    t=[]
    for p,(e1) in enumerate((1,3)):
        t.append(L.send(tok.at[p], X.at[p, L.z], L.dev("z",e1)))
    blocks=[]
    def v0a(xs,ys): return None
    G=[G0,G1,G2]
    pieces0=[(f, (lambda f: lambda xs,ys: G0.at[c,xs,ys,:,pl.ds(f*128,128)])(f)) for f in range(3)]
    pieces0.append((3, lambda xs,ys: G0.at[c,xs,ys,:,pl.ds(384,384)]))
    pieces1=[(f, (lambda f: lambda xs,ys: G1.at[c,xs,ys,:,pl.ds(f*384,384)])(f)) for f in range(4)]
    pieces2=[(f, (lambda f: lambda xs,ys: G2.at[c,xs,ys,pl.ds(f*48,48),:])(f)) for f in range(4)]
    def wait(cps):
        for q in cps: q.wait_recv()
    cps={}
    def start(g, s): cps[g]=gather_step(L, [pieces0,pieces1,pieces2][g], s)
    def sibsend(g, region_step, coords):
        out=[]
        for f,view in [pieces0,pieces1,pieces2][g]:
            for xs,ys,*_ in regions(L, f, region_step, coords):
                out.append(L.send(view(xs,ys), view(xs,ys), L.sib))
        return out
    for (cp,lc) in s0[:2]: cp.wait_recv(); lc.wait()
    G0[c,L.x,L.y,:,0:384]=f0a[...].astype(BF)
    G0[c,L.x,L.y,:,384:768]=f0b[...].astype(BF)
    start(0,0)
    cp,lc=s0[2]; cp.wait_recv(); lc.wait()
    G1[c,L.x,L.y]=f1[...].astype(BF)
    start(1,0)
    cp,lc=s0[3]; cp.wait_recv(); lc.wait()
    G2[c,L.x,L.y]=f2[...].astype(BF)
    start(2,0)
    small_finish(0); small_start(1)
    lt.wait()
    for q in t: q.wait_recv()
    t2=[]
    for p,(e1,e2) in enumerate(((1,3),(3,1))):
        t2.append(L.send(X.at[p, L.z], X.at[p, L.z], L.dev("z",e2)))
        t2.append(L.send(X.at[p, L.at("z",e1)], X.at[p, L.at("z",e1)], L.dev("z",e2)))
    sib=[]
    me={"x":L.x,"y":L.y}
    for s in range(1,4):
        small_finish(s)
        small_start(s+1)
        for g in range(3):
            wait(cps[g]); start(g,s)
            if s==3: sib+=sibsend(g,3,me)
    for g in range(3):
        wait(cps[g])
        out=[]
        for f,view in [pieces0,pieces1,pieces2][g]:
            ax,k=ORDERS[f][3]
            o=dict(me); o[ax]=L.at(ax,k)
            for xs,ys,*_ in regions(L, f, 3, o):
                sib.append(L.send(view(xs,ys), view(xs,ys), L.sib))
    small_finish(4)
    SM[...]=sbuf[0]
    wait(sib); wait(t2)
    L.drain()


def gather(w,wout,wexp,wshr,tok,sm):
    V=pl.BlockSpec(memory_space=pltpu.VMEM); A=pl.BlockSpec(memory_space=pl.ANY)
    S=jax.ShapeDtypeStruct
    return pl.pallas_call(gather_kernel, out_shape=[S((2,4,4,48,768),BF),S((2,4,4,48,1536),BF),S((2,4,4,192,384),BF),S((2,4,128,768),BF),S((16,768),F32)],
      in_specs=[A]*5+[V], out_specs=[V]*5,
      scratch_shapes=[pltpu.VMEM((6,16,768),F32),pltpu.VMEM((48,384),F32),pltpu.VMEM((48,384),F32),pltpu.VMEM((48,1536),F32),pltpu.VMEM((192,384),F32),
        pltpu.SemaphoreType.DMA((160,)),pltpu.SemaphoreType.DMA((160,)),pltpu.SemaphoreType.DMA((5,))],
      compiler_params=pltpu.CompilerParams(collective_id=0, has_side_effects=True, vmem_limit_bytes=50*2**20),
    )(w,wout,wexp,wshr,tok,sm)


SH=((48,768),(48,1536),(192,384))
def scatter_kernel(g0,g1,g2,sm,o0,oi,o1,o2,os_, A0,A1,A2,S0,S1,S2,*rest):
    R=[rest[0:4],rest[4:8],rest[8:12]]
    zi,z0,z1,z2,fi,f0,f1,f2,sbuf,ss,rs,ls=rest[12:]
    L=Links(ss, rs)
    c=L.core
    devs=[L.sib]+[L.dev(a,k) for a in "xyz" for k in (1,3)]
    L.barrier(devs)
    A=[A0,A1,A2]; S=[S0,S1,S2]; g=[g0,g1,g2]
    mine=[]
    for i in range(3):
        cp=pltpu.make_async_copy(g[i],A[i],ls.at[i]); cp.start(); mine.append(cp)
    sbuf[0]=sm[...]
    small=[]
    stages=[L.sib]+[L.dev(a,k) for a,k in (("y",1),("y",3),("x",1),("x",3),("z",1),("z",3))]
    def small_start(i): small.append(L.send(sbuf.at[0], sbuf.at[i+1], stages[i]))
    def small_finish(i):
        small[i].wait_recv(); L.sent(small[i])
        sbuf[0]=sbuf[0]+sbuf[i+1]
    small_start(0)
    sc=[]
    sibs=[]
    order=(2,1,0)
    for i in order:
        mine[i].wait()
        sibs.append(L.send(A[i].at[1-c], S[i], L.sib))
    def mk(i):
        pcs=[(f,(lambda sub: lambda xs,ys: sub(A[i].at[c,xs,ys]))(sub),sub) for f,sub in PIECES[i]]
        return Scatter(L,pcs,R[i])
    sc=[mk(i) for i in range(3)]
    for n,i in enumerate(order):
        sibs[n].wait_recv()
        @pl.loop(0,16)
        def _(k):
            x,y=k//4,k%4
            A[i][c,x,y]=(A[i][c,x,y].astype(F32)+S[i][x,y].astype(F32)).astype(BF)
        sc[i].start(0)
    small_finish(0)
    for s in range(4):
        small_start(s+1)
        for i in order:
            sc[i].finish(s)
            if s<3: sc[i].start(s+1)
        small_finish(s+1)
    x,y=L.x,L.y
    zb=[z0,z1,z2]
    zi[L.z]=A[0][c,x,y,:,0:384]
    V=[A0.at[c,x,y,:,pl.ds(384,384)],A1.at[c,x,y],A2.at[c,x,y]]
    CUT=[(lanes(0,128),lanes(128,256)),(lanes(0,768),lanes(768,768)),(rows(0,96),rows(96,96))]
    zc=[]
    small_start(5)
    for i in order:
        for h,k in enumerate((1,3)):
            zc.append(L.send(CUT[i][h](V[i]), CUT[i][h](zb[i].at[0]), L.dev("z",k)))
    zc.append(L.send(zi.at[L.z], zi.at[L.z], L.dev("z",1)))
    n=0
    zc2=[]
    for i in order:
        for h,k in enumerate((3,1)):
            zc[n].wait_recv(); L.sent(zc[n]); n+=1
            v=CUT[i][h](V[i])
            v[...]=(v[...].astype(F32)+CUT[i][h](zb[i].at[0])[...].astype(F32)).astype(BF)
            zc2.append(L.send(v, CUT[i][h](zb[i].at[1]), L.dev("z",k)))
    zc[n].wait_recv()
    for q in (L.z, L.at("z",1)): zc2.append(L.send(zi.at[q], zi.at[q], L.dev("z",3)))
    small_finish(5); small_start(6)
    n=0
    fb=[f0,f1,f2]
    for i in order:
        for h in range(2):
            zc2[n].wait_recv(); n+=1
            v=CUT[i][h](V[i])
            CUT[i][h](fb[i])[...]=v[...].astype(F32)+CUT[i][h](zb[i].at[1])[...].astype(F32)
    zc2[n].wait_recv(); zc2[n+1].wait_recv()
    fi[...]=zi[...].astype(F32)
    small_finish(6)
    fin=[]; loc=[]
    def rowsend(src, dst, nr, k):
        oth=pl.multiple_of((1-c)*nr,8); own=pl.multiple_of(c*nr,8)
        fin.append(L.send(src.at[...,pl.ds(oth,nr),:], dst.at[c], L.sib))
        lc=pltpu.make_async_copy(src.at[...,pl.ds(own,nr),:], dst.at[c], ls.at[k]); lc.start(); loc.append(lc)
    rowsend(f2,o2,96,2); rowsend(f1,o1,24,1); rowsend(f0,o0,24,0); rowsend(fi,oi,24,3)
    os_[...]=sbuf[0]
    for q in fin: q.wait_recv()
    for q in loc: q.wait()
    L.drain()

NS=120
def scatter(g0,g1,g2,sm):
    V=pl.BlockSpec(memory_space=pltpu.VMEM); A=pl.BlockSpec(memory_space=pl.ANY)
    S=jax.ShapeDtypeStruct
    scr=[pltpu.VMEM((2,4,4)+s,BF) for s in SH]+[pltpu.VMEM((4,4)+s,BF) for s in SH]
    for s in SH: scr+=[pltpu.VMEM((2,4)+s,BF),pltpu.VMEM((4,)+s,BF),pltpu.VMEM((2,)+s,BF),pltpu.VMEM(s,BF)]
    scr+=[pltpu.VMEM((4,48,384),BF),pltpu.VMEM((2,48,384),BF),pltpu.VMEM((2,48,1536),BF),pltpu.VMEM((2,192,384),BF)]
    scr+=[pltpu.VMEM((4,48,384),F32),pltpu.VMEM((48,384),F32),pltpu.VMEM((48,1536),F32),pltpu.VMEM((192,384),F32)]
    scr+=[pltpu.VMEM((8,16,768),F32)]
    return pl.pallas_call(scatter_kernel, out_shape=[S((2,24,384),F32),S((2,4,24,384),F32),S((2,24,1536),F32),S((2,96,384),F32),S((16,768),F32)],
      in_specs=[A,A,A,V], out_specs=[V]*5,
      scratch_shapes=scr+[pltpu.SemaphoreType.DMA((NS,)),pltpu.SemaphoreType.DMA((NS,)),pltpu.SemaphoreType.DMA((5,))],
      compiler_params=pltpu.CompilerParams(collective_id=1, has_side_effects=True, vmem_limit_bytes=56*2**20),
    )(g0,g1,g2,sm)


def spread(vectors, bias, me):
    base = jnp.zeros((12, 768), F32)
    base = lax.dynamic_update_slice(base, vectors.T, (0, me * 24))
    flat = lax.dynamic_update_slice(jnp.zeros((3072,), F32), bias, (me * 96,))
    return jnp.concatenate([base[:8], flat.reshape(4, 768), base[8:]], 0).astype(BF).astype(F32)


def dot(a, b, dims):
    return lax.dot_general(a, b, (dims, ((), ())), preferred_element_type=F32)


NN = ((1,), (0,))
NT = ((1,), (1,))
TN = ((0,), (0,))


def norm_stats(v):
    center = v - jnp.mean(v, -1, keepdims=True)
    r = lax.rsqrt(jnp.mean(center * center, -1, keepdims=True) + norm_eps)
    return center * r, r


def norm_back(z, xhat, r, g):
    zg = z * g
    return r * (zg - jnp.mean(zg, -1, keepdims=True) - xhat * jnp.mean(zg * xhat, -1, keepdims=True))


def body(tokens, cotangent, lengths, input_weight, output_weight, expand_weight, shrink_weight, vectors, expand_bias, *state):
    me = lax.axis_index("fsdp")
    z = lax.axis_index("ctx")
    w = lax.dynamic_slice_in_dim(input_weight.reshape(24, 3, 768), z * 192, 192, 2)
    w = jnp.concatenate([w.reshape(24, 576), jnp.zeros((24, 192), F32)], 1)
    G0, G1, G2, X, sm = gather(w, output_weight, expand_weight, shrink_weight, tokens, spread(vectors, expand_bias, me))
    G0 = G0.reshape(2, 768, 768)
    G1 = G1.reshape(2, 768, 1536)
    G2 = G2.reshape(2, 3072, 384)
    win = jnp.concatenate([G0[0, :, :384], G0[1, :, :192]], 1)
    wout = jnp.concatenate([G0[0, :, 384:], G0[1, :, 384:]], 1)
    wexp = jnp.concatenate([G1[0], G1[1]], 1)
    wshr = jnp.concatenate([G2[0], G2[1]], 1)
    g1, b1, bq, bv, bo, g2, b2, bd = [sm[i : i + 1] for i in range(8)]
    bias = sm[8:12].reshape(1, 3072)
    ends = jnp.cumsum(lengths, axis=1)
    pos = jnp.arange(512)
    segment = jnp.sum((pos[None, :, None] >= ends[:, None, :]).astype(jnp.int32), axis=2)
    live = (lax.dynamic_slice_in_dim(segment, z * 128, 128, 1) < 4).astype(F32).reshape(256, 1)
    xhat, r = norm_stats(X.reshape(1024, 768).astype(F32))
    normed = (xhat * g1 + b1).astype(BF)
    proj = dot(normed, win, NN)
    wq = lax.dynamic_slice_in_dim(bq, z * 192, 192, 1)
    wv = lax.dynamic_slice_in_dim(bv, z * 192, 192, 1)
    heads = lambda v: v.astype(BF).reshape(2, 512, 3, 64)
    q, k, v = heads(proj[:, :192] + wq), heads(proj[:, 192:384]), heads(proj[:, 384:] + wv)
    es = lambda e, a, b: jnp.einsum(e, a, b, preferred_element_type=F32)
    s = es("pqhd,pkhd->phqk", q, k) * 0.125
    ok = (segment[:, :, None] == segment[:, None, :]) & (pos[None, None, :] <= pos[None, :, None])
    s = jnp.where(ok[:, None], s, -1e30)
    e = jnp.exp(s - jnp.max(s, -1, keepdims=True))
    p32 = e / jnp.sum(e, -1, keepdims=True)
    p = p32.astype(BF)
    ctx = es("phqk,pkhd->pqhd", p, v).astype(BF).reshape(2, 4, 128, 192)
    context = lax.all_to_all(ctx, "ctx", 1, 2).reshape(256, 768)
    x = tokens.reshape(256, 768).astype(F32)
    after = x + (dot(context, wout, NN) + bo)
    xhat2, r2 = norm_stats(after)
    second = (xhat2 * g2 + b2).astype(BF)
    expanded = dot(second, wexp, NN) + bias
    cdf = 0.5 * (1.0 + lax.erf(expanded * (2.0 ** -0.5)))
    hidden = (expanded * cdf).astype(BF)
    slope = cdf + expanded * (jnp.exp(-0.5 * expanded * expanded) * 0.3989422804014327)
    out = ((after + dot(hidden, wshr, NN) + bd) * live).astype(BF).reshape(2, 128, 768)
    up = cotangent.reshape(256, 768) * live.astype(BF)
    up32 = up.astype(F32)
    d_shr = dot(hidden, up, TN)
    eb = (dot(up, wshr, NT) * slope).astype(BF)
    d_exp = dot(second, eb, TN)
    sb = dot(eb, wexp, NT)
    resid = up32 + norm_back(sb, xhat2, r2, g2)
    ab = resid.astype(BF)
    d_out = dot(context, ab, TN)
    cb = dot(ab, wout, NT).astype(BF).reshape(2, 128, 4, 192)
    do = lax.all_to_all(cb, "ctx", 2, 1).reshape(2, 512, 3, 64)
    dv = es("phqk,pqhd->pkhd", p, do)
    dp = es("pqhd,pkhd->phqk", do, v)
    ds = (p32 * (dp - jnp.sum(p32 * dp, -1, keepdims=True))).astype(BF)
    dq = es("phqk,pkhd->pqhd", ds, k) * 0.125
    dk = es("phqk,pqhd->pkhd", ds, q) * 0.125
    pb = jnp.concatenate([a.astype(BF).reshape(1024, 192) for a in (dq, dk, dv)], 1)
    d_in = dot(normed, pb, TN)
    nb = dot(pb, win, NT).astype(BF).reshape(2, 4, 128, 768)
    nb = jnp.sum(lax.all_to_all(nb, "ctx", 1, 0).astype(F32), 0).reshape(256, 768)
    xh, rr = norm_stats(x)
    tokens_gradient = (resid + norm_back(nb, xh, rr, g1)).reshape(2, 128, 768)
    col = lambda a: jnp.sum(a, 0)
    row = jnp.zeros((2, 768), F32)
    pbs = col(pb.astype(F32))
    row = lax.dynamic_update_slice(row, jnp.stack([pbs[:192], pbs[384:]]), (0, z * 192))
    smg = jnp.concatenate([jnp.stack([col(nb * xh), col(nb), row[0], row[1], col(ab.astype(F32)), col(sb * xhat2), col(sb), col(up32)]),
        col(eb.astype(F32)).reshape(4, 768), jnp.zeros((4, 768), F32)], 0)
    d_in = jnp.concatenate([d_in, jnp.zeros((768, 192), F32)], 1)
    cut = lambda a, n: a.astype(BF).reshape(-1, 2, n).transpose(1, 0, 2)
    GR0 = jnp.concatenate([cut(d_in, 384), cut(d_out, 384)], 2).reshape(2, 4, 4, 48, 768)
    GR1 = cut(d_exp, 1536).reshape(2, 4, 4, 48, 1536)
    GR2 = cut(d_shr, 384).reshape(2, 4, 4, 192, 384)
    o0, oi, o1, o2, os_ = scatter(GR0, GR1, GR2, smg)
    join = lambda a: jnp.moveaxis(a, 0, -2).reshape(a.shape[1:-1] + (-1,))
    full = join(oi)[:, :, :576].reshape(4, 24, 3, 192).transpose(1, 2, 0, 3).reshape(24, 2304)
    vec = lax.dynamic_slice_in_dim(os_[:8], me * 24, 24, 1).T
    bia = lax.dynamic_slice_in_dim(os_[8:12].reshape(3072), me * 96, 96, 0)
    grads = (full, join(o0), join(o1), join(o2), vec, bia)
    weights = (input_weight, output_weight, expand_weight, shrink_weight, vectors, expand_bias)
    rates = (2.0 * D ** (-0.5), 4.0 * D ** (-0.5), 2.0 * D ** (-0.5), 2.0 * FF ** (-0.5), 1.0, 1.0)
    new = [adam_step(weights[i], grads[i], state[i], state[6 + i], rates[i]) for i in range(6)]
    return (out, tokens_gradient) + tuple(n[j] for j in range(3) for n in new)


def solution(mesh):
    in_specs = (
        P("fsdp", "ctx", None),
        P("fsdp", "ctx", None),
        P("fsdp", None),
        P("fsdp", None),
        P("fsdp", None),
        P("fsdp", None),
        P("fsdp", None),
        P("fsdp", None),
        P("fsdp"),
        P("fsdp", None),
        P("fsdp", None),
        P("fsdp", None),
        P("fsdp", None),
        P("fsdp", None),
        P("fsdp"),
        P("fsdp", None),
        P("fsdp", None),
        P("fsdp", None),
        P("fsdp", None),
        P("fsdp", None),
        P("fsdp"),
    )
    out_specs = (
        P("fsdp", "ctx", None),
        P("fsdp", "ctx", None),
        P("fsdp", None),
        P("fsdp", None),
        P("fsdp", None),
        P("fsdp", None),
        P("fsdp", None),
        P("fsdp"),
        P("fsdp", None),
        P("fsdp", None),
        P("fsdp", None),
        P("fsdp", None),
        P("fsdp", None),
        P("fsdp"),
        P("fsdp", None),
        P("fsdp", None),
        P("fsdp", None),
        P("fsdp", None),
        P("fsdp", None),
        P("fsdp"),
    )
    return jax.shard_map(body, mesh=mesh, in_specs=in_specs, out_specs=out_specs, check_vma=False)
```

```python
import jax, jax.numpy as jnp
from jax import lax
from jax.experimental import pallas as pl
from jax.experimental.pallas import tpu as pltpu
from jax.sharding import PartitionSpec as P

MESH = pl.DeviceIdType.MESH
BF = jnp.bfloat16
F32 = jnp.float32


def flip1(v):
    return v + 1 - 2 * (v % 2)


class Links:
    def __init__(self, send_sems, recv_sems):
        self.send_sems, self.recv_sems, self.used = send_sems, recv_sems, 0
        me = lax.axis_index("fsdp")
        self.z = lax.axis_index("ctx")
        self.core = me % 2
        self.chip = me // 2
        self.x, self.y = self.chip // 4, self.chip % 4
        self.sib = {"fsdp": me + 1 - 2 * self.core}
        self.pending = []

    def at(self, axis, kind):
        v = {"x": self.x, "y": self.y, "z": self.z}[axis]
        return flip1(v) if kind == 1 else 3 - v

    def dev(self, axis, kind):
        if axis == "z":
            return {"ctx": self.at("z", kind)}
        x = self.at("x", kind) if axis == "x" else self.x
        y = self.at("y", kind) if axis == "y" else self.y
        return {"fsdp": (x * 4 + y) * 2 + self.core}

    def send(self, src, dst, device):
        i = self.used
        self.used += 1
        copy = pltpu.make_async_remote_copy(
            src_ref=src, dst_ref=dst, send_sem=self.send_sems.at[i],
            recv_sem=self.recv_sems.at[i], device_id=device, device_id_type=MESH,
        )
        copy.start()
        self.pending.append(copy)
        return copy

    def barrier(self, devices):
        sem = pltpu.get_barrier_semaphore()
        for d in devices:
            pl.semaphore_signal(sem, inc=1, device_id=d, device_id_type=MESH)
        pl.semaphore_wait(sem, len(devices))

    def sent(self, copy):
        copy.wait_send()
        self.pending = [q for q in self.pending if q is not copy]

    def drain(self):
        for c in self.pending:
            c.wait_send()
        self.pending = []


ORDERS = (
    (("y", 1), ("y", 3), ("x", 1), ("x", 3)),
    (("y", 3), ("y", 1), ("x", 3), ("x", 1)),
    (("x", 1), ("x", 3), ("y", 1), ("y", 3)),
    (("x", 3), ("x", 1), ("y", 3), ("y", 1)),
)


def held(v, kind, count):
    if count == 0:
        return [(v, 1)]
    if count == 2:
        return [(0, 4)]
    if kind == 1:
        return [(v - v % 2, 2)]
    return [(v, 1), (3 - v, 1)]


def regions(links, flavor, step, coords):
    order = ORDERS[flavor]
    first, second = order[0][0], order[2][0]
    a = held(coords[first], order[0][1], min(step, 2))
    b = held(coords[second], order[2][1], max(step - 2, 0))
    out = []
    for i, (sa, na) in enumerate(a):
        for j, (sb, nb) in enumerate(b):
            sel = {first: pl.ds(sa, na), second: pl.ds(sb, nb)}
            out.append((sel["x"], sel["y"], i, j, {first: na, second: nb}))
    return out


def gather_step(links, pieces, step):
    copies = []
    for flavor, view in pieces:
        axis, kind = ORDERS[flavor][step]
        device = links.dev(axis, kind)
        for xs, ys, *_ in regions(links, flavor, step, {"x": links.x, "y": links.y}):
            copies.append(links.send(view(xs, ys), view(xs, ys), device))
    return copies


def pair_of(v, kind):
    if kind == 1:
        return [v - v % 2, v - v % 2 + 1]
    return [v, 3 - v]


class Scatter:
    def __init__(self, links, pieces, bufs):
        self.links, self.pieces, self.bufs = links, pieces, bufs

    def _sel(self, flavor, a, b):
        first = ORDERS[flavor][0][0]
        return (a, b) if first == "x" else (b, a)

    def start(self, step):
        L = self.links
        self.copies = []
        for flavor, acc, sub in self.pieces:
            order = ORDERS[flavor]
            axis, kind = order[3 - step]
            first, second = order[0][0], order[2][0]
            va, vb = {"x": L.x, "y": L.y}[first], {"x": L.x, "y": L.y}[second]
            p = L.at(axis, kind)
            dev = L.dev(axis, kind)
            if step == 0:
                for j, b in enumerate(pair_of(p, order[2][1])):
                    self.copies.append(L.send(acc(*self._sel(flavor, pl.ds(0, 4), b)), sub(self.bufs[0].at[j]), dev))
            elif step == 1:
                self.copies.append(L.send(acc(*self._sel(flavor, pl.ds(0, 4), p)), sub(self.bufs[1]), dev))
            elif step == 2:
                for j, a in enumerate(pair_of(p, order[0][1])):
                    self.copies.append(L.send(acc(*self._sel(flavor, a, vb)), sub(self.bufs[2].at[j]), dev))
            else:
                self.copies.append(L.send(acc(*self._sel(flavor, p, vb)), sub(self.bufs[3]), dev))

    def finish(self, step):
        L = self.links
        for c in self.copies:
            c.wait_recv()

        def add(view, buf):
            view[...] = (view[...].astype(F32) + buf[...].astype(F32)).astype(BF)

        for flavor, acc, sub in self.pieces:
            order = ORDERS[flavor]
            first, second = order[0][0], order[2][0]
            va, vb = {"x": L.x, "y": L.y}[first], {"x": L.x, "y": L.y}[second]
            if step == 0:
                for j, b in enumerate(pair_of(vb, order[2][1])):
                    for a in range(4):
                        add(acc(*self._sel(flavor, a, b)), sub(self.bufs[0].at[j, a]))
            elif step == 1:
                for a in range(4):
                    add(acc(*self._sel(flavor, a, vb)), sub(self.bufs[1].at[a]))
            elif step == 2:
                for j, a in enumerate(pair_of(va, order[0][1])):
                    add(acc(*self._sel(flavor, a, vb)), sub(self.bufs[2].at[j]))
            else:
                add(acc(*self._sel(flavor, va, vb)), sub(self.bufs[3]))


def lanes(n, size):
    return lambda ref: ref.at[..., pl.ds(n, size)]


def rows(n, size):
    return lambda ref: ref.at[..., pl.ds(n, size), :]


PIECES = (
    tuple((f, lanes(f * 128, 128)) for f in range(3)) + ((3, lanes(384, 384)),),
    tuple((f, lanes(f * 384, 384)) for f in range(4)),
    tuple((f, rows(f * 48, 48)) for f in range(4)),
)


D = 768
H = 12
HD = 64
FF = 3072
STEP = 10


norm_eps = 1e-05
beta_first = 0.9
beta_second = 0.999
adam_eps = 1e-08
decay_rate = 0.01


def adam_step(weight, gradient, moment, square, rate):
    moment_new = beta_first * moment + (1.0 - beta_first) * gradient
    square_new = beta_second * square + (1.0 - beta_second) * gradient * gradient
    corrected = moment_new / (1.0 - beta_first**STEP)
    spread = jnp.sqrt(square_new / (1.0 - beta_second**STEP)) + adam_eps
    return (weight - rate * (corrected / spread + decay_rate * weight), moment_new, square_new)


NN = ((1,), (0,))
NT = ((1,), (1,))
TN = ((0,), (0,))


def dot(a, b, dims):
    return lax.dot_general(a, b, (dims, ((), ())), preferred_element_type=F32)


def norm_stats(v):
    center = v - jnp.mean(v, -1, keepdims=True)
    r = lax.rsqrt(jnp.mean(center * center, -1, keepdims=True) + norm_eps)
    return center * r, r


def norm_back(z, xhat, r, g):
    zg = z * g
    return r * (zg - jnp.mean(zg, -1, keepdims=True) - xhat * jnp.mean(zg * xhat, -1, keepdims=True))


def colsum(v):
    return jnp.sum(v, 0, keepdims=True)


SHAPES = ((48, 768), (48, 1536), (192, 384))


def layer_kernel(
    lengths, tok_hbm, tok, cot, win, wout, wexp, wshr, sm,
    out, tgrad, o0, oi, o1, o2, osm,
    f0a, f0b, f1, f2, sbuf, gbuf,
    G0, G1, G2, A0, A1, A2, S0, S1, S2,
    R00, R01, R02, R03, R10, R11, R12, R13, R20, R21, R22, R23,
    zi, z0, z1, z2, fi, f0f, f1f, f2f,
    X, QK, V, P, MB, CS, CT, after, xh2, r2, second, sect, hidden, slope, up, ab, CBS, CB, PQK, PV, N1, N2,
    ss, rs, ls,
):
    L = Links(ss, rs)
    c, z, x, y = L.core, L.z, L.x, L.y
    me = {"x": x, "y": y}
    zf, zt, zo = L.at("z", 1), L.at("z", 3), (z + 2) % 4
    zpeers = (zf, zt, zo)
    L.barrier([L.sib] + [L.dev(a, k) for a in "xyz" for k in (1, 3)] + [{"ctx": zo}])
    G, A, S = [G0, G1, G2], [A0, A1, A2], [S0, S1, S2]

    def wait(copies):
        for q in copies:
            q.wait_recv()

    local = [0]

    def move(src, dst):
        cp = pltpu.make_async_copy(src, dst, ls.at[local[0]])
        local[0] += 1
        cp.start()
        return cp

    stages = [L.sib] + [L.dev(a, k) for a, k in (("y", 1), ("y", 3), ("x", 1), ("x", 3), ("z", 1), ("z", 3))]

    class Sum:
        def __init__(self, buf):
            self.buf = buf

        def start(self, i):
            self.copy = L.send(self.buf.at[0], self.buf.at[i + 1], stages[i])

        def finish(self, i):
            self.copy.wait_recv()
            L.sent(self.copy)
            self.buf[0] = self.buf[0] + self.buf[i + 1]

    small = Sum(sbuf)
    sbuf[0] = sm[...]
    small.start(0)

    def halves(src, n, dst, nr):
        other, mine = pl.multiple_of((1 - c) * n, 128), pl.multiple_of(c * n, 128)
        r = pl.ds(pl.multiple_of(nr * c, 8), nr)
        return L.send(src.at[:, pl.ds(other, n)], dst.at[r], L.sib), move(src.at[:, pl.ds(mine, n)], dst.at[r])

    pairs = [halves(win, 384, f0a, 24), halves(wout, 384, f0b, 24)]
    xl = move(tok_hbm, X.at[:, z])
    tz = []
    for p in range(2):
        for h, k in enumerate((1, 3)):
            r = pl.ds(h * 64, 64)
            tz.append(L.send(tok_hbm.at[p, r], X.at[p, z, r], L.dev("z", k)))
    pairs += [halves(wexp, 1536, f1, 24), halves(wshr, 384, f2, 96)]

    views = []
    for g in range(3):
        views.append([(f, (lambda sub, g: lambda xs, ys: sub(G[g].at[c, xs, ys]))(sub, g)) for f, sub in PIECES[g]])
    flight = {}

    def start(g, s):
        flight[g] = gather_step(L, views[g], s)

    def advance(g, s):
        wait(flight[g])
        start(g, s)

    def to_sibling(g, arrived):
        res = []
        for f, view in views[g]:
            axis, kind = ORDERS[f][3]
            o = dict(me)
            if arrived:
                o[axis] = L.at(axis, kind)
            for xs, ys, *_ in regions(L, f, 3, o):
                res.append(L.send(view(xs, ys), view(xs, ys), L.sib))
        return res

    for cp, lc in pairs[:2]:
        cp.wait_recv()
        lc.wait()
    G0[c, x, y, :, 0:384] = f0a[...].astype(BF)
    G0[c, x, y, :, 384:768] = f0b[...].astype(BF)
    start(0, 0)
    small.finish(0)
    small.start(1)
    for g, f in ((1, f1), (2, f2)):
        cp, lc = pairs[g + 1]
        cp.wait_recv()
        lc.wait()
        G[g][c, x, y] = f[...].astype(BF)
        start(g, 0)
    advance(0, 1)
    small.finish(1)
    small.start(2)
    xl.wait()
    tz2 = []
    for p in range(2):
        for h, (k1, k2) in enumerate(((1, 3), (3, 1))):
            r = pl.ds(h * 64, 64)
            tz[2 * p + h].wait_recv()
            q = L.at("z", k1)
            tz2.append([L.send(X.at[p, b, r], X.at[p, b, r], L.dev("z", k2)) for b in (z, q)])
    advance(0, 2)
    small.finish(2)
    small.start(3)
    advance(1, 1)
    advance(2, 1)
    advance(0, 3)
    sib = {0: to_sibling(0, False)}
    small.finish(3)
    small.start(4)

    seqs = lengths.shape[1]

    def segment(p, shape, dim):
        pos = lax.broadcasted_iota(jnp.int32, shape, dim)
        end = lengths[p, 0]
        seg = (pos >= end).astype(jnp.int32)
        for i in range(1, seqs):
            end = end + lengths[p, i]
            seg = seg + (pos >= end).astype(jnp.int32)
        return seg

    def fill_mask(p):
        ok = segment(p, (512, 1), 0) == segment(p, (1, 512), 1)
        ok = ok & (lax.broadcasted_iota(jnp.int32, (512, 512), 1) <= lax.broadcasted_iota(jnp.int32, (512, 512), 0))
        MB[...] = jnp.where(ok, 0.0, -1e30)

    def live_rows(p):
        pos = lax.broadcasted_iota(jnp.int32, (128, 1), 0) + z * 128
        total = lengths[p, 0]
        for i in range(1, seqs):
            total = total + lengths[p, i]
        return (pos < total).astype(F32)

    small.finish(4)
    g1, b1 = sbuf[0, 0:1], sbuf[0, 1:2]

    def ready(p):
        for q in tz2[2 * p] + tz2[2 * p + 1]:
            q.wait_recv()
            L.sent(q)

    def project(p):
        for b in range(4):
            xhat, _ = norm_stats(X[p, b].astype(F32))
            X[p, b] = (xhat * g1 + b1).astype(BF)

    def qkv(p):
        n = X[p].reshape(512, 768)
        qk = dot(n, G0[0, :, :, :, 0:384].reshape(768, 384), NN)
        q = (qk[:, 0:192] + sbuf[0, 12:13, 0:192]) * 0.125
        QK[p] = jnp.concatenate([q, qk[:, 192:384]], 1).astype(BF)
        V[p] = (dot(n, G0[1, :, :, :, 0:256].reshape(768, 256), NN) + sbuf[0, 13:14, 0:256]).astype(BF)

    def attend(p):
        parts = [[], []]
        for h in range(3):
            q = QK[p, :, h * 64 : h * 64 + 64]
            k = QK[p, :, 192 + h * 64 : 256 + h * 64]
            v = V[p, :, h * 64 : h * 64 + 64]
            for i in range(2):
                r, n = i * 256, (i + 1) * 256
                s = dot(q[r : r + 256], k[:n], NT) + MB[r : r + 256, 0:n]
                e = jnp.exp(s - jnp.max(s, -1, keepdims=True))
                pr = (e * (1.0 / jnp.sum(e, -1, keepdims=True))).astype(BF)
                P[p * 3 + h, r : r + 256, 0:n] = pr
                parts[i].append(dot(pr, v[:n], NN))
        for i in range(2):
            ctx = jnp.concatenate(parts[i], 1).astype(BF)
            CS[p, 2 * i : 2 * i + 2] = ctx.reshape(2, 128, 192)

    def to_heads_owner(p, src, dst):
        res = [L.send(src.at[p, q], dst.at[z, p], {"ctx": q}) for q in zpeers]
        return res

    ready(0)
    project(0)
    wait(flight[0])
    sib[0] += to_sibling(0, True)
    advance(1, 2)
    advance(2, 2)
    fill_mask(0)
    wait(sib[0])
    qkv(0)
    attend(0)
    ctx_moves = to_heads_owner(0, CS, CT)
    own = [move(CS.at[0, z], CT.at[z, 0])]
    advance(1, 3)
    sib[1] = to_sibling(1, False)
    advance(2, 3)
    sib[2] = to_sibling(2, False)
    ready(1)
    project(1)
    fill_mask(1)
    qkv(1)
    attend(1)
    ctx_moves += to_heads_owner(1, CS, CT)
    own.append(move(CS.at[1, z], CT.at[z, 1]))
    wait(flight[1])
    sib[1] += to_sibling(1, True)
    wait(flight[2])
    sib[2] += to_sibling(2, True)
    for q in own:
        q.wait()
    wait(ctx_moves)

    bo, g2, b2, bd = sbuf[0, 4:5], sbuf[0, 5:6], sbuf[0, 6:7], sbuf[0, 7:8]
    for h in range(2):
        acc = sbuf[0, 4:5, h * 384 : h * 384 + 384] + tok[:, :, h * 384 : h * 384 + 384].astype(F32).reshape(256, 384)
        for q in range(4):
            acc = acc + dot(CT[q].reshape(256, 192), G0[h, q, :, :, 384:768].reshape(192, 384), NN)
        after[:, h * 384 : h * 384 + 384] = acc
    xhat, r = norm_stats(after[...])
    xh2[...] = xhat
    r2[...] = r
    sec = (xhat * g2 + b2).astype(BF)
    second[...] = sec
    sect[...] = sec.T
    live = [live_rows(p) for p in range(2)]
    for p in range(2):
        up[p * 128 : p * 128 + 128] = cot[p] * live[p].astype(BF)

    wait(sib[1])
    for t in range(4):
        lane = (t % 2) * 768
        e = dot(second[...], G1[t // 2, :, :, :, lane : lane + 768].reshape(768, 768), NN) + sbuf[0, 8 + t : 9 + t]
        cdf = 0.5 * (1.0 + lax.erf(e * (2.0 ** -0.5)))
        hidden[:, t * 768 : t * 768 + 768] = (e * cdf).astype(BF)
        slope[:, t * 768 : t * 768 + 768] = (cdf + e * (jnp.exp(-0.5 * e * e) * 0.3989422804014327)).astype(BF)
    wait(sib[2])

    for t in range(4):
        for h in range(2):
            d = dot(hidden[:, t * 768 : t * 768 + 768], up[:, h * 384 : h * 384 + 384], TN)
            A2[h, t] = d.astype(BF).reshape(4, 192, 384)

    def pieces_of(i):
        return [(f, (lambda sub: lambda xs, ys: sub(A[i].at[c, xs, ys]))(sub), sub) for f, sub in PIECES[i]]

    bufs = [[R00, R01, R02, R03], [R10, R11, R12, R13], [R20, R21, R22, R23]]
    sc = [Scatter(L, pieces_of(i), bufs[i]) for i in range(3)]
    pair = {}

    def pair_start(i):
        pair[i] = L.send(A[i].at[1 - c], S[i], L.sib)

    def pair_finish(i):
        pair[i].wait_recv()

        @pl.loop(0, 4)
        def _(k):
            A[i][c, k] = (A[i][c, k].astype(F32) + S[i][k].astype(F32)).astype(BF)

        sc[i].start(0)

    def turn(i, s):
        sc[i].finish(s)
        if s < 3:
            sc[i].start(s + 1)

    pair_start(2)

    for h in range(2):
        w = after[:, h * 384 : h * 384 + 384] + bd[:, h * 384 : h * 384 + 384]
        for t in range(4):
            w = w + dot(hidden[:, t * 768 : t * 768 + 768], G2[h, t].reshape(768, 384), NN)
        for p in range(2):
            out[p, :, h * 384 : h * 384 + 384] = (w[p * 128 : p * 128 + 128] * live[p]).astype(BF)
    pair_finish(2)

    resid = after
    gsum = Sum(gbuf)
    for t in range(4):
        lane = (t % 2) * 768
        cols = pl.ds(t * 768, 768)
        hb = dot(up[:, 0:384], G2[0, t].reshape(768, 384), NT) + dot(up[:, 384:768], G2[1, t].reshape(768, 384), NT)
        eb = (hb * slope[:, cols].astype(F32)).astype(BF)
        hidden[:, cols] = eb
        gbuf[0, 8 + t : 9 + t] = colsum(eb.astype(F32))
        part = dot(eb, G1[t // 2, :, :, :, lane : lane + 768].reshape(768, 768), NT)
        if t == 0:
            resid[...] = part
        else:
            resid[...] += part
        for q in range(4):
            d = dot(sect[q * 192 : q * 192 + 192], eb, NN).astype(BF)
            A1[t // 2, q, :, :, lane : lane + 768] = d.reshape(4, 48, 768)
    pair_start(1)
    turn(2, 0)
    sb = resid[...]
    gbuf[0, 5:6] = colsum(sb * xh2[...])
    gbuf[0, 6:7] = colsum(sb)
    up32 = up[...].astype(F32)
    gbuf[0, 7:8] = colsum(up32)
    res = up32 + norm_back(sb, xh2[...], r2[...], g2)
    resid[...] = res
    ab[...] = res.astype(BF)
    gbuf[0, 4:5] = colsum(ab[...].astype(F32))

    for q in range(4):
        d = dot(ab[:, 0:384], G0[0, q, :, :, 384:768].reshape(192, 384), NT)
        d = d + dot(ab[:, 384:768], G0[1, q, :, :, 384:768].reshape(192, 384), NT)
        CBS[:, q] = d.astype(BF).reshape(2, 128, 192)
    back_moves = [to_heads_owner(p, CBS, CB) for p in range(2)]
    own = [move(CBS.at[p, z], CB.at[z, p]) for p in range(2)]
    for q in range(4):
        d = dot(CT[q].reshape(256, 192), ab[...], TN).astype(BF)
        for h in range(2):
            A0[h, q, :, :, 384:768] = d[:, h * 384 : h * 384 + 384].reshape(4, 48, 384)
    pair_finish(1)
    turn(2, 1)

    def attend_back(p):
        co = CB[:, p].reshape(512, 192)
        dqs, dks, dvs = [[], []], [], []
        for h in range(3):
            do = co[:, h * 64 : h * 64 + 64]
            q = QK[p, :, h * 64 : h * 64 + 64]
            k = QK[p, :, 192 + h * 64 : 256 + h * 64]
            v = V[p, :, h * 64 : h * 64 + 64]
            dk, dv = [], []
            for i in range(2):
                r, n = i * 256, (i + 1) * 256
                pr = P[p * 3 + h, r : r + 256, 0:n]
                p32 = pr.astype(F32)
                dp = dot(do[r : r + 256], v[:n], NT)
                ds = (p32 * (dp - jnp.sum(p32 * dp, -1, keepdims=True))).astype(BF)
                dqs[i].append(dot(ds, k[:n], NN) * 0.125)
                dk.append(dot(ds, q[r : r + 256], TN))
                dv.append(dot(pr, do[r : r + 256], TN))
            dks.append([dk[0] + dk[1][:256], dk[1][256:]])
            dvs.append([dv[0] + dv[1][:256], dv[1][256:]])
        for i in range(2):
            r = i * 256
            PQK[p, r : r + 256] = jnp.concatenate(dqs[i] + [d[i] for d in dks], 1).astype(BF)
            PV[p, r : r + 256] = jnp.concatenate([d[i] for d in dvs] + [jnp.zeros((256, 64), F32)], 1).astype(BF)

    def NB(p, b):
        lane = b * 768 if isinstance(b, int) else pl.multiple_of(b * 768, 128)
        return hidden.at[pl.ds(p * 128, 128), pl.ds(lane, 768)]

    nb_moves = [None, None]
    kinds = ((1, 3), (3, 1))

    def inner_back(p):
        n = dot(PQK[p], G0[0, :, :, :, 0:384].reshape(768, 384), NT)
        n = n + dot(PV[p], G0[1, :, :, :, 0:256].reshape(768, 256), NT)
        for b in range(4):
            NB(p, b)[...] = n[b * 128 : b * 128 + 128].astype(BF)
        k1, k2 = kinds[p]
        q = L.at("z", k1)
        nb_moves[p] = [L.send(NB(p, b), N1.at[p, j], L.dev("z", k1)) for j, b in enumerate((q, zo if k2 != k1 else q))]

    for p in range(2):
        own[p].wait()
        wait(back_moves[p])
        attend_back(p)
        inner_back(p)
        turn(2, 2 + p)
        if p == 0:
            turn(1, 0)
    for q in range(2):
        xs, n = slice(2 * q, 2 * q + 2), X[:, :, :, q * 384 : q * 384 + 384].reshape(1024, 384)
        A0[0, xs, :, :, 0:384] = dot(n, PQK[...].reshape(1024, 384), TN).astype(BF).reshape(2, 4, 48, 384)
        A0[1, xs, :, :, 0:256] = dot(n, PV[...].reshape(1024, 256), TN).astype(BF).reshape(2, 4, 48, 256)
    A0[1, :, :, :, 256:384] = jnp.zeros((4, 4, 48, 128), BF)
    pair_start(0)
    gbuf[0, 0:4] = jnp.zeros((4, 768), F32)
    gbuf[0, 12:16] = jnp.zeros((4, 768), F32)
    mine = lax.broadcasted_iota(jnp.int32, (4, 1), 0) == z
    sq = colsum(PQK[...].reshape(1024, 384)[:, 0:256].astype(F32))
    sv = colsum(PV[...].reshape(1024, 256).astype(F32))
    gbuf[0, 12:16, 0:256] = jnp.where(mine, sq, 0.0)
    gbuf[0, 12:16, 256:512] = jnp.where(mine, sv, 0.0)
    turn(1, 1)

    second_moves = []
    for p in range(2):
        k1, k2 = kinds[p]
        wait(nb_moves[p])
        q = L.at("z", k2)
        NB(p, q)[...] = (NB(p, q)[...].astype(F32) + N1[p, 1].astype(F32)).astype(BF)
        second_moves.append(L.send(NB(p, q), N2.at[p], L.dev("z", k2)))
    pair_finish(0)
    turn(1, 2)
    for p in range(2):
        second_moves[p].wait_recv()
        rows_p = slice(p * 128, p * 128 + 128)
        nb = NB(p, z)[...].astype(F32) + N1[p, 0].astype(F32) + N2[p].astype(F32)
        xhat, r = norm_stats(tok[p].astype(F32))
        tgrad[p] = resid[rows_p] + norm_back(nb, xhat, r, g1)
        gbuf[0, 0:1] += colsum(nb * xhat)
        gbuf[0, 1:2] += colsum(nb)
    gsum.start(0)
    turn(0, 0)
    turn(1, 3)

    zb = [z0, z1, z2]
    W = [A0.at[c, x, y, :, pl.ds(384, 384)], A1.at[c, x, y], A2.at[c, x, y]]
    CUT = [(lanes(0, 128), lanes(128, 256)), (lanes(0, 768), lanes(768, 768)), (rows(0, 96), rows(96, 96))]
    zc, zc2 = {}, {}

    def z_start(i):
        zc[i] = [L.send(CUT[i][h](W[i]), CUT[i][h](zb[i].at[0]), L.dev("z", k)) for h, k in enumerate((1, 3))]

    def z_turn(i):
        zc2[i] = []
        for h, k in enumerate((3, 1)):
            q = zc[i][h]
            q.wait_recv()
            L.sent(q)
            v = CUT[i][h](W[i])
            v[...] = (v[...].astype(F32) + CUT[i][h](zb[i].at[0])[...].astype(F32)).astype(BF)
            zc2[i].append(L.send(v, CUT[i][h](zb[i].at[1]), L.dev("z", k)))

    fin, loc = [], []

    def hand(src, dst, nr):
        oth, ours = pl.multiple_of((1 - c) * nr, 8), pl.multiple_of(c * nr, 8)
        fin.append(L.send(src.at[..., pl.ds(oth, nr), :], dst.at[c], L.sib))
        loc.append(move(src.at[..., pl.ds(ours, nr), :], dst.at[c]))

    def z_finish(i, f, o, nr):
        for h in range(2):
            zc2[i][h].wait_recv()
            CUT[i][h](f)[...] = CUT[i][h](W[i])[...].astype(F32) + CUT[i][h](zb[i].at[1])[...].astype(F32)
        hand(f, o, nr)

    z_start(2)
    z_start(1)
    gsum.finish(0)
    gsum.start(1)
    turn(0, 1)
    z_turn(2)
    z_turn(1)
    gsum.finish(1)
    gsum.start(2)
    turn(0, 2)
    gsum.finish(2)
    gsum.start(3)
    turn(0, 3)
    z_start(0)
    zi[z] = A0[c, x, y, :, 0:384]
    zic = L.send(zi.at[z], zi.at[z], L.dev("z", 1))
    z_finish(2, f2f, o2, 96)
    z_finish(1, f1f, o1, 24)
    gsum.finish(3)
    gsum.start(4)
    z_turn(0)
    zic.wait_recv()
    zic2 = [L.send(zi.at[q], zi.at[q], L.dev("z", 3)) for q in (z, zf)]
    gsum.finish(4)
    gsum.start(5)
    z_finish(0, f0f, o0, 24)
    wait(zic2)
    fi[...] = zi[...].astype(F32)
    hand(fi, oi, 24)
    gsum.finish(5)
    gsum.start(6)
    wait(fin)
    for q in loc:
        q.wait()
    gsum.finish(6)
    osm[...] = gbuf[0]
    L.drain()


def layer(lengths, tokens, cot, w, wout, wexp, wshr, sm):
    V = pl.BlockSpec(memory_space=pltpu.VMEM)
    A = pl.BlockSpec(memory_space=pl.ANY)
    M = pl.BlockSpec(memory_space=pltpu.SMEM)
    S = jax.ShapeDtypeStruct
    b = lambda *s: pltpu.VMEM(s, BF)
    f = lambda *s: pltpu.VMEM(s, F32)
    scratch = [f(48, 384), f(48, 384), f(48, 1536), f(192, 384), f(6, 16, 768), f(8, 16, 768)]
    scratch += [b(2, 4, 4, *s) for s in SHAPES] * 2 + [b(4, 4, *s) for s in SHAPES]
    for s in SHAPES:
        scratch += [b(2, 4, *s), b(4, *s), b(2, *s), b(*s)]
    scratch += [b(4, 48, 384), b(2, 48, 384), b(2, 48, 1536), b(2, 192, 384)]
    scratch += [f(4, 48, 384), f(48, 384), f(48, 1536), f(192, 384)]
    scratch += [
        b(2, 4, 128, 768), b(2, 512, 384), b(2, 512, 256), b(6, 512, 512), f(512, 512),
        b(2, 4, 128, 192), b(4, 2, 128, 192), f(256, 768), f(256, 768), f(256, 1), b(256, 768), b(768, 256),
        b(256, 3072), b(256, 3072), b(256, 768), b(256, 768), b(2, 4, 128, 192), b(4, 2, 128, 192),
        b(2, 512, 384), b(2, 512, 256), b(2, 2, 128, 768), b(2, 128, 768),
    ]
    n = 300
    scratch += [pltpu.SemaphoreType.DMA((n,)), pltpu.SemaphoreType.DMA((n,)), pltpu.SemaphoreType.DMA((16,))]
    return pl.pallas_call(
        layer_kernel,
        out_shape=[
            S((2, 128, 768), BF), S((2, 128, 768), F32),
            S((2, 24, 384), F32), S((2, 4, 24, 384), F32), S((2, 24, 1536), F32), S((2, 96, 384), F32), S((16, 768), F32),
        ],
        in_specs=[M, A, V, V, A, A, A, A, V],
        out_specs=[V] * 7,
        scratch_shapes=scratch,
        compiler_params=pltpu.CompilerParams(collective_id=0, has_side_effects=True, vmem_limit_bytes=63 * 2**20),
        cost_estimate=pl.CostEstimate(flops=13 * 10**9, bytes_accessed=10**7, transcendentals=10**7),
    )(lengths, tokens, tokens, cot, w, wout, wexp, wshr, sm)


def spread(vectors, bias, me, z):
    base = lax.dynamic_update_slice(jnp.zeros((8, 768), F32), vectors.T, (0, me * 24))
    flat = lax.dynamic_update_slice(jnp.zeros((3072,), F32), bias, (me * 96,))
    part = lax.dynamic_slice(base, (2, z * 192), (2, 192))
    part = jnp.concatenate([part, jnp.zeros((2, 576), F32)], 1)
    return jnp.concatenate([base, flat.reshape(4, 768), part, jnp.zeros((2, 768), F32)], 0).astype(BF).astype(F32)


def body(tokens, cotangent, lengths, input_weight, output_weight, expand_weight, shrink_weight, vectors, expand_bias, *state):
    me = lax.axis_index("fsdp")
    z = lax.axis_index("ctx")
    w = lax.dynamic_slice_in_dim(input_weight.reshape(24, 3, 768), z * 192, 192, 2)
    w = jnp.concatenate([w.reshape(24, 576), jnp.zeros((24, 192), F32)], 1)
    small = spread(vectors, expand_bias, me, z)
    out, tokens_gradient, o0, oi, o1, o2, os_ = layer(
        lengths, tokens, cotangent, w, output_weight, expand_weight, shrink_weight, small
    )
    join = lambda a: jnp.moveaxis(a, 0, -2).reshape(a.shape[1:-1] + (-1,))
    full = join(oi)[:, :, :576].reshape(4, 24, 3, 192).transpose(1, 2, 0, 3).reshape(24, 2304)
    heads = os_[12:16, 0:512].reshape(4, 2, 256)[:, :, :192].transpose(1, 0, 2).reshape(2, 768)
    rows8 = jnp.concatenate([os_[0:2], heads, os_[4:8]], 0)
    vec = lax.dynamic_slice_in_dim(rows8, me * 24, 24, 1).T
    bia = lax.dynamic_slice_in_dim(os_[8:12].reshape(3072), me * 96, 96, 0)
    grads = (full, join(o0), join(o1), join(o2), vec, bia)
    weights = (input_weight, output_weight, expand_weight, shrink_weight, vectors, expand_bias)
    rates = (2.0 * D ** (-0.5), 4.0 * D ** (-0.5), 2.0 * D ** (-0.5), 2.0 * FF ** (-0.5), 1.0, 1.0)
    new = [adam_step(weights[i], grads[i], state[i], state[6 + i], rates[i]) for i in range(6)]
    return (out, tokens_gradient) + tuple(n[j] for j in range(3) for n in new)


def solution(mesh):
    in_specs = (
        P("fsdp", "ctx", None),
        P("fsdp", "ctx", None),
        P("fsdp", None),
        P("fsdp", None),
        P("fsdp", None),
        P("fsdp", None),
        P("fsdp", None),
        P("fsdp", None),
        P("fsdp"),
        P("fsdp", None),
        P("fsdp", None),
        P("fsdp", None),
        P("fsdp", None),
        P("fsdp", None),
        P("fsdp"),
        P("fsdp", None),
        P("fsdp", None),
        P("fsdp", None),
        P("fsdp", None),
        P("fsdp", None),
        P("fsdp"),
    )
    out_specs = (
        P("fsdp", "ctx", None),
        P("fsdp", "ctx", None),
        P("fsdp", None),
        P("fsdp", None),
        P("fsdp", None),
        P("fsdp", None),
        P("fsdp", None),
        P("fsdp"),
        P("fsdp", None),
        P("fsdp", None),
        P("fsdp", None),
        P("fsdp", None),
        P("fsdp", None),
        P("fsdp"),
        P("fsdp", None),
        P("fsdp", None),
        P("fsdp", None),
        P("fsdp", None),
        P("fsdp", None),
        P("fsdp"),
    )
    return jax.shard_map(body, mesh=mesh, in_specs=in_specs, out_specs=out_specs, check_vma=False)
```

```python
import jax, jax.numpy as jnp
from jax import lax
from jax.experimental import pallas as pl
from jax.experimental.pallas import tpu as pltpu
from jax.sharding import PartitionSpec as P

MESH = pl.DeviceIdType.MESH
BF = jnp.bfloat16
F32 = jnp.float32


def flip1(v):
    return v + 1 - 2 * (v % 2)


class Links:
    def __init__(self, send_sems, recv_sems):
        self.send_sems, self.recv_sems, self.used = send_sems, recv_sems, 0
        me = lax.axis_index("fsdp")
        self.z = lax.axis_index("ctx")
        self.core = me % 2
        self.chip = me // 2
        self.x, self.y = self.chip // 4, self.chip % 4
        self.sib = {"fsdp": me + 1 - 2 * self.core}
        self.pending = []

    def at(self, axis, kind):
        v = {"x": self.x, "y": self.y, "z": self.z}[axis]
        return flip1(v) if kind == 1 else 3 - v

    def dev(self, axis, kind):
        if axis == "z":
            return {"ctx": self.at("z", kind)}
        x = self.at("x", kind) if axis == "x" else self.x
        y = self.at("y", kind) if axis == "y" else self.y
        return {"fsdp": (x * 4 + y) * 2 + self.core}

    def peers(self, axis):
        v = {"x": self.x, "y": self.y, "z": self.z}[axis]
        others = [flip1(v), 3 - v, (v + 2) % 4]
        if axis == "z":
            return [{"ctx": o} for o in others]
        if axis == "x":
            return [{"fsdp": (o * 4 + self.y) * 2 + self.core} for o in others]
        return [{"fsdp": (self.x * 4 + o) * 2 + self.core} for o in others]

    def send(self, src, dst, device):
        i = self.used
        self.used += 1
        copy = pltpu.make_async_remote_copy(
            src_ref=src, dst_ref=dst, send_sem=self.send_sems.at[i],
            recv_sem=self.recv_sems.at[i], device_id=device, device_id_type=MESH,
        )
        copy.start()
        self.pending.append(copy)
        return copy

    def barrier(self, devices):
        sem = pltpu.get_barrier_semaphore()
        for d in devices:
            pl.semaphore_signal(sem, inc=1, device_id=d, device_id_type=MESH)
        pl.semaphore_wait(sem, len(devices))

    def sent(self, copy):
        copy.wait_send()
        self.pending = [q for q in self.pending if q is not copy]

    def drain(self):
        for c in self.pending:
            c.wait_send()
        self.pending = []


ORDERS = (
    (("y", 1), ("y", 3), ("x", 1), ("x", 3)),
    (("y", 3), ("y", 1), ("x", 3), ("x", 1)),
    (("x", 1), ("x", 3), ("y", 1), ("y", 3)),
    (("x", 3), ("x", 1), ("y", 3), ("y", 1)),
)


def held(v, kind, count):
    if count == 0:
        return [(v, 1)]
    if count == 2:
        return [(0, 4)]
    if kind == 1:
        return [(v - v % 2, 2)]
    return [(v, 1), (3 - v, 1)]


def regions(links, flavor, step, coords):
    order = ORDERS[flavor]
    first, second = order[0][0], order[2][0]
    a = held(coords[first], order[0][1], min(step, 2))
    b = held(coords[second], order[2][1], max(step - 2, 0))
    out = []
    for i, (sa, na) in enumerate(a):
        for j, (sb, nb) in enumerate(b):
            sel = {first: pl.ds(sa, na), second: pl.ds(sb, nb)}
            out.append((sel["x"], sel["y"], i, j, {first: na, second: nb}))
    return out


def gather_step(links, pieces, step):
    copies = []
    for flavor, view in pieces:
        axis, kind = ORDERS[flavor][step]
        device = links.dev(axis, kind)
        for xs, ys, *_ in regions(links, flavor, step, {"x": links.x, "y": links.y}):
            copies.append(links.send(view(xs, ys), view(xs, ys), device))
    return copies


def pair_of(v, kind):
    if kind == 1:
        return [v - v % 2, v - v % 2 + 1]
    return [v, 3 - v]


class Scatter:
    def __init__(self, links, pieces, bufs):
        self.links, self.pieces, self.bufs = links, pieces, bufs

    def _sel(self, flavor, a, b):
        first = ORDERS[flavor][0][0]
        return (a, b) if first == "x" else (b, a)

    def start(self, step):
        L = self.links
        self.copies = []
        for flavor, acc, sub in self.pieces:
            order = ORDERS[flavor]
            axis, kind = order[3 - step]
            first, second = order[0][0], order[2][0]
            va, vb = {"x": L.x, "y": L.y}[first], {"x": L.x, "y": L.y}[second]
            p = L.at(axis, kind)
            dev = L.dev(axis, kind)
            if step == 0:
                for j, b in enumerate(pair_of(p, order[2][1])):
                    self.copies.append(L.send(acc(*self._sel(flavor, pl.ds(0, 4), b)), sub(self.bufs[0].at[j]), dev))
            elif step == 1:
                self.copies.append(L.send(acc(*self._sel(flavor, pl.ds(0, 4), p)), sub(self.bufs[1]), dev))
            elif step == 2:
                for j, a in enumerate(pair_of(p, order[0][1])):
                    self.copies.append(L.send(acc(*self._sel(flavor, a, vb)), sub(self.bufs[2].at[j]), dev))
            else:
                self.copies.append(L.send(acc(*self._sel(flavor, p, vb)), sub(self.bufs[3]), dev))

    def finish(self, step):
        L = self.links
        for c in self.copies:
            c.wait_recv()

        def add(view, buf):
            view[...] = (view[...].astype(F32) + buf[...].astype(F32)).astype(BF)

        for flavor, acc, sub in self.pieces:
            order = ORDERS[flavor]
            first, second = order[0][0], order[2][0]
            va, vb = {"x": L.x, "y": L.y}[first], {"x": L.x, "y": L.y}[second]
            if step == 0:
                for j, b in enumerate(pair_of(vb, order[2][1])):
                    for a in range(4):
                        add(acc(*self._sel(flavor, a, b)), sub(self.bufs[0].at[j, a]))
            elif step == 1:
                for a in range(4):
                    add(acc(*self._sel(flavor, a, vb)), sub(self.bufs[1].at[a]))
            elif step == 2:
                for j, a in enumerate(pair_of(va, order[0][1])):
                    add(acc(*self._sel(flavor, a, vb)), sub(self.bufs[2].at[j]))
            else:
                add(acc(*self._sel(flavor, va, vb)), sub(self.bufs[3]))


def lanes(n, size):
    return lambda ref: ref.at[..., pl.ds(n, size)]


def rows(n, size):
    return lambda ref: ref.at[..., pl.ds(n, size), :]


PIECES = (
    tuple((f, lanes(f * 128, 128)) for f in range(3)) + tuple((3 - f, lanes(384 + f * 128, 128)) for f in range(3)),
    tuple((f, lanes(f * 384, 384)) for f in range(4)),
    tuple((f, rows(f * 48, 48)) for f in range(4)),
)


D = 768
H = 12
HD = 64
FF = 3072
STEP = 10


norm_eps = 1e-05
beta_first = 0.9
beta_second = 0.999
adam_eps = 1e-08
decay_rate = 0.01


def adam_step(weight, gradient, moment, square, rate):
    moment_new = beta_first * moment + (1.0 - beta_first) * gradient
    square_new = beta_second * square + (1.0 - beta_second) * gradient * gradient
    corrected = moment_new / (1.0 - beta_first**STEP)
    spread = jnp.sqrt(square_new / (1.0 - beta_second**STEP)) + adam_eps
    return (weight - rate * (corrected / spread + decay_rate * weight), moment_new, square_new)


NN = ((1,), (0,))
NT = ((1,), (1,))
TN = ((0,), (0,))


def dot(a, b, dims):
    return lax.dot_general(a, b, (dims, ((), ())), preferred_element_type=F32)


def norm_stats(v):
    center = v - jnp.mean(v, -1, keepdims=True)
    r = lax.rsqrt(jnp.mean(center * center, -1, keepdims=True) + norm_eps)
    return center * r, r


def norm_back(z, xhat, r, g):
    zg = z * g
    return r * (zg - jnp.mean(zg, -1, keepdims=True) - xhat * jnp.mean(zg * xhat, -1, keepdims=True))


def colsum(v):
    return jnp.sum(v, 0, keepdims=True)


SHAPES = ((48, 768), (48, 1536), (192, 384))


def layer_kernel(
    lengths, tok, cot, win_all, wout, wexp, wshr, vecs, bias_in,
    out, tgrad, o0, oi, o1, o2, osm,
    win, f0a, f0b, f1, f2, sbuf, gbuf,
    G0, G1, G2, A0, A1, A2, S0, S1, S2,
    R00, R01, R02, R03, R10, R11, R12, R13, R20, R21, R22, R23,
    zi, z0, z1, z2, fi, f0f, f1f, f2f,
    X, QK, V, P, MB, CS, CT, after, xh2, r2, second, sect, hidden, slope, up, ab, CBS, CB, PQK, PV, N1, N2,
    ss, rs, ls,
):
    L = Links(ss, rs)
    c, z, x, y = L.core, L.z, L.x, L.y
    me = {"x": x, "y": y}
    zf, zt, zo = L.at("z", 1), L.at("z", 3), (z + 2) % 4
    zpeers = (zf, zt, zo)
    G, A, S = [G0, G1, G2], [A0, A1, A2], [S0, S1, S2]

    def wait(copies):
        for q in copies:
            q.wait_recv()

    local = [0]

    def move(src, dst):
        cp = pltpu.make_async_copy(src, dst, ls.at[local[0]])
        local[0] += 1
        cp.start()
        return cp

    class Sum:
        def __init__(self, buf):
            self.buf = buf

        def start(self, axis):
            base = 1 + 4 * "cyxz".index(axis)
            v, to = {"c": (c, [L.sib]), "x": (x, L.peers("x")), "y": (y, L.peers("y")), "z": (z, L.peers("z"))}[axis]
            self.buf[base + v] = self.buf[0]
            self.slots = [base + i for i in range(len(to) + 1)]
            self.copies = [L.send(self.buf.at[base + v], self.buf.at[base + v], d) for d in to]

        def finish(self):
            wait(self.copies)
            total = self.buf[self.slots[0]]
            for i in self.slots[1:]:
                total = total + self.buf[i]
            self.buf[0] = total

    small = Sum(sbuf)
    me_all = lax.axis_index("fsdp")
    tiled = vecs[...]
    for _ in range(5):
        tiled = jnp.concatenate([tiled, tiled], 1)
    lane = lax.broadcasted_iota(jnp.int32, (1, 768), 1)
    first = me_all * 24
    sbuf[0] = jnp.zeros((16, 768), F32)
    sbuf[0, 0:8] = jnp.where((lane >= first) & (lane < first + 24), tiled, 0.0)
    near = (lane + z * 192 >= first) & (lane + z * 192 < first + 24) & (lane < 192)
    sbuf[0, 12:14] = jnp.where(near, tiled[2:4], 0.0)
    tiled = jnp.broadcast_to(bias_in[...], (4, 96))
    for _ in range(3):
        tiled = jnp.concatenate([tiled, tiled], 1)
    first = (me_all % 8) * 96
    here = (lax.broadcasted_iota(jnp.int32, (4, 1), 0) == me_all // 8) & (lane >= first) & (lane < first + 96)
    sbuf[0, 8:12] = jnp.where(here, tiled, 0.0)
    sbuf[0] = sbuf[0].astype(BF).astype(F32)
    for j in range(3):
        cut = [win_all[:, j * 768 + q * 192 : j * 768 + q * 192 + 192] for q in range(4)]
        win[:, j * 192 : j * 192 + 192] = jnp.where(z == 0, cut[0], jnp.where(z == 1, cut[1], jnp.where(z == 2, cut[2], cut[3])))
    win[:, 576:768] = jnp.zeros((24, 192), F32)
    L.barrier([L.sib] + L.peers("x") + L.peers("y") + L.peers("z"))
    small.start("c")

    def halves(src, n, dst, nr):
        other, mine = pl.multiple_of((1 - c) * n, 128), pl.multiple_of(c * n, 128)
        r = pl.ds(pl.multiple_of(nr * c, 8), nr)
        return L.send(src.at[:, pl.ds(other, n)], dst.at[r], L.sib), move(src.at[:, pl.ds(mine, n)], dst.at[r])

    pairs = [halves(win, 384, f0a, 24), halves(wout, 384, f0b, 24)]
    xl = move(tok, X.at[:, z])
    tz = []
    for p in range(2):
        for h, k in enumerate((1, 3)):
            r = pl.ds(h * 64, 64)
            tz.append(L.send(tok.at[p, r], X.at[p, z, r], L.dev("z", k)))
    pairs += [halves(wexp, 1536, f1, 24), halves(wshr, 384, f2, 96)]

    views = []
    for g in range(3):
        views.append([(f, (lambda sub, g: lambda xs, ys: sub(G[g].at[c, xs, ys]))(sub, g)) for f, sub in PIECES[g]])
    flight = {}

    def start(g, s):
        flight[g] = gather_step(L, views[g], s)

    def advance(g, s):
        wait(flight[g])
        start(g, s)

    def to_sibling(g, arrived):
        res = []
        for f, view in views[g]:
            axis, kind = ORDERS[f][3]
            o = dict(me)
            if arrived:
                o[axis] = L.at(axis, kind)
            for xs, ys, *_ in regions(L, f, 3, o):
                res.append(L.send(view(xs, ys), view(xs, ys), L.sib))
        return res

    for cp, lc in pairs[:2]:
        cp.wait_recv()
        lc.wait()
    G0[c, x, y, :, 0:384] = f0a[...].astype(BF)
    G0[c, x, y, :, 384:768] = f0b[...].astype(BF)
    start(0, 0)
    small.finish()
    small.start("y")
    for g, f in ((1, f1), (2, f2)):
        cp, lc = pairs[g + 1]
        cp.wait_recv()
        lc.wait()
        G[g][c, x, y] = f[...].astype(BF)
        start(g, 0)
    advance(0, 1)
    small.finish()
    small.start("x")
    xl.wait()
    tz2 = []
    for p in range(2):
        for h, (k1, k2) in enumerate(((1, 3), (3, 1))):
            r = pl.ds(h * 64, 64)
            tz[2 * p + h].wait_recv()
            q = L.at("z", k1)
            tz2.append([L.send(X.at[p, b, r], X.at[p, b, r], L.dev("z", k2)) for b in (z, q)])
    advance(0, 2)
    advance(1, 1)
    advance(2, 1)
    advance(0, 3)
    sib = {0: to_sibling(0, False)}

    seqs = lengths.shape[1]

    def segment(p, shape, dim):
        pos = lax.broadcasted_iota(jnp.int32, shape, dim)
        end = lengths[p, 0]
        seg = (pos >= end).astype(jnp.int32)
        for i in range(1, seqs):
            end = end + lengths[p, i]
            seg = seg + (pos >= end).astype(jnp.int32)
        return seg

    def fill_mask(p):
        ok = segment(p, (512, 1), 0) == segment(p, (1, 512), 1)
        ok = ok & (lax.broadcasted_iota(jnp.int32, (512, 512), 1) <= lax.broadcasted_iota(jnp.int32, (512, 512), 0))
        MB[...] = jnp.where(ok, 0.0, -1e30)

    def live_rows(p):
        pos = lax.broadcasted_iota(jnp.int32, (128, 1), 0) + z * 128
        total = lengths[p, 0]
        for i in range(1, seqs):
            total = total + lengths[p, i]
        return (pos < total).astype(F32)

    small.finish()
    g1, b1 = sbuf[0, 0:1], sbuf[0, 1:2]

    def ready(p):
        for q in tz2[2 * p] + tz2[2 * p + 1]:
            q.wait_recv()
            L.sent(q)

    def project(p):
        for b in range(4):
            xhat, _ = norm_stats(X[p, b].astype(F32))
            X[p, b] = (xhat * g1 + b1).astype(BF)

    def qkv(p):
        n = X[p].reshape(512, 768)
        qk = dot(n, G0[0, :, :, :, 0:384].reshape(768, 384), NN)
        q = (qk[:, 0:192] + sbuf[0, 12:13, 0:192]) * 0.125
        QK[p] = jnp.concatenate([q, qk[:, 192:384]], 1).astype(BF)
        V[p] = (dot(n, G0[1, :, :, :, 0:256].reshape(768, 256), NN) + sbuf[0, 13:14, 0:256]).astype(BF)

    def attend(p):
        parts = [[], []]
        for h in range(3):
            q = QK[p, :, h * 64 : h * 64 + 64]
            k = QK[p, :, 192 + h * 64 : 256 + h * 64]
            v = V[p, :, h * 64 : h * 64 + 64]
            for i in range(2):
                r, n = i * 256, (i + 1) * 256
                s = dot(q[r : r + 256], k[:n], NT) + MB[r : r + 256, 0:n]
                e = jnp.exp(s - jnp.max(s, -1, keepdims=True))
                pr = (e * (1.0 / jnp.sum(e, -1, keepdims=True))).astype(BF)
                P[p * 3 + h, r : r + 256, 0:n] = pr
                parts[i].append(dot(pr, v[:n], NN))
        for i in range(2):
            ctx = jnp.concatenate(parts[i], 1).astype(BF)
            CS[p, 2 * i : 2 * i + 2] = ctx.reshape(2, 128, 192)

    def to_heads_owner(p, src, dst):
        res = [L.send(src.at[p, q], dst.at[z, p], {"ctx": q}) for q in zpeers]
        return res

    ready(0)
    project(0)
    wait(flight[0])
    sib[0] += to_sibling(0, True)
    advance(1, 2)
    advance(2, 2)
    fill_mask(0)
    wait(sib[0])
    qkv(0)
    attend(0)
    ctx_moves = to_heads_owner(0, CS, CT)
    own = [move(CS.at[0, z], CT.at[z, 0])]
    advance(1, 3)
    sib[1] = to_sibling(1, False)
    advance(2, 3)
    sib[2] = to_sibling(2, False)
    ready(1)
    project(1)
    fill_mask(1)
    qkv(1)
    attend(1)
    ctx_moves += to_heads_owner(1, CS, CT)
    own.append(move(CS.at[1, z], CT.at[z, 1]))
    wait(flight[1])
    sib[1] += to_sibling(1, True)
    for q in own:
        q.wait()
    wait(ctx_moves)

    bo, g2, b2, bd = sbuf[0, 4:5], sbuf[0, 5:6], sbuf[0, 6:7], sbuf[0, 7:8]
    for h in range(2):
        acc = sbuf[0, 4:5, h * 384 : h * 384 + 384] + tok[:, :, h * 384 : h * 384 + 384].astype(F32).reshape(256, 384)
        for q in range(4):
            acc = acc + dot(CT[q].reshape(256, 192), G0[h, q, :, :, 384:768].reshape(192, 384), NN)
        after[:, h * 384 : h * 384 + 384] = acc
    xhat, r = norm_stats(after[...])
    xh2[...] = xhat
    r2[...] = r
    sec = (xhat * g2 + b2).astype(BF)
    second[...] = sec
    sect[...] = sec.T
    live = [live_rows(p) for p in range(2)]
    for p in range(2):
        up[p * 128 : p * 128 + 128] = cot[p] * live[p].astype(BF)

    wait(sib[1])
    for t in range(4):
        lane = (t % 2) * 768
        e = dot(second[...], G1[t // 2, :, :, :, lane : lane + 768].reshape(768, 768), NN) + sbuf[0, 8 + t : 9 + t]
        cdf = 0.5 * (1.0 + lax.erf(e * (2.0 ** -0.5)))
        hidden[:, t * 768 : t * 768 + 768] = (e * cdf).astype(BF)
        slope[:, t * 768 : t * 768 + 768] = (cdf + e * (jnp.exp(-0.5 * e * e) * 0.3989422804014327)).astype(BF)
    for t in range(4):
        for h in range(2):
            d = dot(hidden[:, t * 768 : t * 768 + 768], up[:, h * 384 : h * 384 + 384], TN)
            A2[h, t] = d.astype(BF).reshape(4, 192, 384)

    def pieces_of(i):
        return [(f, (lambda sub: lambda xs, ys: sub(A[i].at[c, xs, ys]))(sub), sub) for f, sub in PIECES[i]]

    bufs = [[R00, R01, R02, R03], [R10, R11, R12, R13], [R20, R21, R22, R23]]
    sc = {1: Scatter(L, pieces_of(1), bufs[1]), 2: Scatter(L, pieces_of(2), bufs[2])}
    sc["in"] = Scatter(L, pieces_of(0)[:3], bufs[0])
    sc["out"] = Scatter(L, pieces_of(0)[3:], bufs[0])
    pair = {}
    split = {"in": lanes(0, 384), "out": lanes(384, 384)}

    def pair_start(i):
        if i in split:
            pair[i] = L.send(split[i](A0.at[1 - c]), split[i](S0), L.sib)
        else:
            pair[i] = L.send(A[i].at[1 - c], S[i], L.sib)

    def pair_finish(i):
        pair[i].wait_recv()

        @pl.loop(0, 4)
        def _(k):
            if i in split:
                a, b = split[i](A0.at[c, k]), split[i](S0.at[k])
            else:
                a, b = A[i].at[c, k], S[i].at[k]
            a[...] = (a[...].astype(F32) + b[...].astype(F32)).astype(BF)

        sc[i].start(0)

    def turn(i, s):
        sc[i].finish(s)
        if s < 3:
            sc[i].start(s + 1)

    pair_start(2)

    wait(flight[2])
    sib[2] += to_sibling(2, True)
    pair_finish(2)
    wait(sib[2])

    for h in range(2):
        w = after[:, h * 384 : h * 384 + 384] + bd[:, h * 384 : h * 384 + 384]
        for t in range(4):
            w = w + dot(hidden[:, t * 768 : t * 768 + 768], G2[h, t].reshape(768, 384), NN)
        for p in range(2):
            out[p, :, h * 384 : h * 384 + 384] = (w[p * 128 : p * 128 + 128] * live[p]).astype(BF)

    resid = after
    gsum = Sum(gbuf)
    for t in range(4):
        lane = (t % 2) * 768
        cols = pl.ds(t * 768, 768)
        hb = dot(up[:, 0:384], G2[0, t].reshape(768, 384), NT) + dot(up[:, 384:768], G2[1, t].reshape(768, 384), NT)
        eb = (hb * slope[:, cols].astype(F32)).astype(BF)
        hidden[:, cols] = eb
        gbuf[0, 8 + t : 9 + t] = colsum(eb.astype(F32))
        part = dot(eb, G1[t // 2, :, :, :, lane : lane + 768].reshape(768, 768), NT)
        if t == 0:
            resid[...] = part
        else:
            resid[...] += part
        for q in range(4):
            d = dot(sect[q * 192 : q * 192 + 192], eb, NN).astype(BF)
            A1[t // 2, q, :, :, lane : lane + 768] = d.reshape(4, 48, 768)
    pair_start(1)
    turn(2, 0)
    sb = resid[...]
    gbuf[0, 5:6] = colsum(sb * xh2[...])
    gbuf[0, 6:7] = colsum(sb)
    up32 = up[...].astype(F32)
    gbuf[0, 7:8] = colsum(up32)
    res = up32 + norm_back(sb, xh2[...], r2[...], g2)
    resid[...] = res
    ab[...] = res.astype(BF)
    gbuf[0, 4:5] = colsum(ab[...].astype(F32))

    for q in range(4):
        d = dot(ab[:, 0:384], G0[0, q, :, :, 384:768].reshape(192, 384), NT)
        d = d + dot(ab[:, 384:768], G0[1, q, :, :, 384:768].reshape(192, 384), NT)
        CBS[:, q] = d.astype(BF).reshape(2, 128, 192)
    back_moves = [to_heads_owner(p, CBS, CB) for p in range(2)]
    own = [move(CBS.at[p, z], CB.at[z, p]) for p in range(2)]
    for q in range(4):
        d = dot(CT[q].reshape(256, 192), ab[...], TN).astype(BF)
        for h in range(2):
            A0[h, q, :, :, 384:768] = d[:, h * 384 : h * 384 + 384].reshape(4, 48, 384)
    pair_start("out")
    pair_finish(1)
    turn(2, 1)
    pair_finish("out")

    def attend_back(p):
        co = CB[:, p].reshape(512, 192)
        dqs, dks, dvs = [[], []], [], []
        for h in range(3):
            do = co[:, h * 64 : h * 64 + 64]
            q = QK[p, :, h * 64 : h * 64 + 64]
            k = QK[p, :, 192 + h * 64 : 256 + h * 64]
            v = V[p, :, h * 64 : h * 64 + 64]
            dk, dv = [], []
            for i in range(2):
                r, n = i * 256, (i + 1) * 256
                pr = P[p * 3 + h, r : r + 256, 0:n]
                p32 = pr.astype(F32)
                dp = dot(do[r : r + 256], v[:n], NT)
                ds = (p32 * (dp - jnp.sum(p32 * dp, -1, keepdims=True))).astype(BF)
                dqs[i].append(dot(ds, k[:n], NN) * 0.125)
                dk.append(dot(ds, q[r : r + 256], TN))
                dv.append(dot(pr, do[r : r + 256], TN))
            dks.append([dk[0] + dk[1][:256], dk[1][256:]])
            dvs.append([dv[0] + dv[1][:256], dv[1][256:]])
        for i in range(2):
            r = i * 256
            PQK[p, r : r + 256] = jnp.concatenate(dqs[i] + [d[i] for d in dks], 1).astype(BF)
            PV[p, r : r + 256] = jnp.concatenate([d[i] for d in dvs] + [jnp.zeros((256, 64), F32)], 1).astype(BF)

    def NB(p, b):
        lane = b * 768 if isinstance(b, int) else pl.multiple_of(b * 768, 128)
        return hidden.at[pl.ds(p * 128, 128), pl.ds(lane, 768)]

    nb_moves = [None, None]
    kinds = ((1, 3), (3, 1))

    def inner_back(p):
        n = dot(PQK[p], G0[0, :, :, :, 0:384].reshape(768, 384), NT)
        n = n + dot(PV[p], G0[1, :, :, :, 0:256].reshape(768, 256), NT)
        for b in range(4):
            NB(p, b)[...] = n[b * 128 : b * 128 + 128].astype(BF)
        k1, k2 = kinds[p]
        q = L.at("z", k1)
        nb_moves[p] = [L.send(NB(p, b), N1.at[p, j], L.dev("z", k1)) for j, b in enumerate((q, zo if k2 != k1 else q))]

    for p in range(2):
        own[p].wait()
        wait(back_moves[p])
        attend_back(p)
        inner_back(p)
        if p == 0:
            turn(2, 2)
            turn(1, 0)
    for q in range(2):
        xs, n = slice(2 * q, 2 * q + 2), X[:, :, :, q * 384 : q * 384 + 384].reshape(1024, 384)
        A0[0, xs, :, :, 0:384] = dot(n, PQK[...].reshape(1024, 384), TN).astype(BF).reshape(2, 4, 48, 384)
        A0[1, xs, :, :, 0:256] = dot(n, PV[...].reshape(1024, 256), TN).astype(BF).reshape(2, 4, 48, 256)
    A0[1, :, :, :, 256:384] = jnp.zeros((4, 4, 48, 128), BF)
    pair_start("in")
    gbuf[0, 0:4] = jnp.zeros((4, 768), F32)
    gbuf[0, 12:16] = jnp.zeros((4, 768), F32)
    mine = lax.broadcasted_iota(jnp.int32, (4, 1), 0) == z
    sq = colsum(PQK[...].reshape(1024, 384)[:, 0:256].astype(F32))
    sv = colsum(PV[...].reshape(1024, 256).astype(F32))
    gbuf[0, 12:16, 0:256] = jnp.where(mine, sq, 0.0)
    gbuf[0, 12:16, 256:512] = jnp.where(mine, sv, 0.0)
    zb = [z0, z1, z2]
    W = [A0.at[c, x, y, :, pl.ds(384, 384)], A1.at[c, x, y], A2.at[c, x, y]]
    CUT = [(lanes(0, 128), lanes(128, 256)), (lanes(0, 768), lanes(768, 768)), (rows(0, 96), rows(96, 96))]
    zc, zc2 = {}, {}

    def z_start(i):
        zc[i] = [L.send(CUT[i][h](W[i]), CUT[i][h](zb[i].at[0]), L.dev("z", k)) for h, k in enumerate((1, 3))]

    def z_turn(i):
        zc2[i] = []
        for h, k in enumerate((3, 1)):
            q = zc[i][h]
            q.wait_recv()
            L.sent(q)
            v = CUT[i][h](W[i])
            v[...] = (v[...].astype(F32) + CUT[i][h](zb[i].at[0])[...].astype(F32)).astype(BF)
            zc2[i].append(L.send(v, CUT[i][h](zb[i].at[1]), L.dev("z", k)))

    fin, loc = [], []

    def hand(src, dst, nr):
        oth, ours = pl.multiple_of((1 - c) * nr, 8), pl.multiple_of(c * nr, 8)
        fin.append(L.send(src.at[..., pl.ds(oth, nr), :], dst.at[c], L.sib))
        loc.append(move(src.at[..., pl.ds(ours, nr), :], dst.at[c]))

    def z_finish(i, f, o, nr):
        for h in range(2):
            zc2[i][h].wait_recv()
            CUT[i][h](f)[...] = CUT[i][h](W[i])[...].astype(F32) + CUT[i][h](zb[i].at[1])[...].astype(F32)
        hand(f, o, nr)

    turn(2, 3)
    z_start(2)
    turn("out", 0)
    turn(1, 1)
    pair_finish("in")
    turn("out", 1)

    second_moves = []
    for p in range(2):
        k1, k2 = kinds[p]
        wait(nb_moves[p])
        q = L.at("z", k2)
        NB(p, q)[...] = (NB(p, q)[...].astype(F32) + N1[p, 1].astype(F32)).astype(BF)
        second_moves.append(L.send(NB(p, q), N2.at[p], L.dev("z", k2)))
    turn(1, 2)
    turn("out", 2)
    turn("in", 0)
    z_turn(2)
    turn(1, 3)
    z_start(1)
    turn("out", 3)
    z_start(0)
    turn("in", 1)
    z_finish(2, f2f, o2, 96)
    turn("in", 2)
    z_turn(1)
    z_turn(0)
    for p in range(2):
        second_moves[p].wait_recv()
        rows_p = slice(p * 128, p * 128 + 128)
        nb = NB(p, z)[...].astype(F32) + N1[p, 0].astype(F32) + N2[p].astype(F32)
        xhat, r = norm_stats(tok[p].astype(F32))
        tgrad[p] = resid[rows_p] + norm_back(nb, xhat, r, g1)
        gbuf[0, 0:1] += colsum(nb * xhat)
        gbuf[0, 1:2] += colsum(nb)
    gsum.start("c")
    turn("in", 3)
    zi[z] = A0[c, x, y, :, 0:384]
    zic = [L.send(zi.at[z], zi.at[z], d) for d in L.peers("z")]
    gsum.finish()
    gsum.start("z")
    z_finish(1, f1f, o1, 24)
    z_finish(0, f0f, o0, 24)
    wait(zic)
    fi[...] = zi[...].astype(F32)
    hand(fi, oi, 24)
    gsum.finish()
    gsum.start("y")
    gsum.finish()
    gsum.start("x")
    wait(fin)
    for q in loc:
        q.wait()
    gsum.finish()
    osm[...] = gbuf[0]
    L.drain()


def layer(lengths, tokens, cot, w, wout, wexp, wshr, vecs, bias_in):
    V = pl.BlockSpec(memory_space=pltpu.VMEM)
    A = pl.BlockSpec(memory_space=pltpu.HBM)
    M = pl.BlockSpec(memory_space=pltpu.SMEM)
    S = jax.ShapeDtypeStruct
    b = lambda *s: pltpu.VMEM(s, BF)
    f = lambda *s: pltpu.VMEM(s, F32)
    scratch = [f(24, 768), f(48, 384), f(48, 384), f(48, 1536), f(192, 384), f(13, 16, 768), f(17, 16, 768)]
    scratch += [b(2, 4, 4, *s) for s in SHAPES] * 2 + [b(4, 4, *s) for s in SHAPES]
    for s in SHAPES:
        scratch += [b(2, 4, *s), b(4, *s), b(2, *s), b(*s)]
    scratch += [b(4, 48, 384), b(2, 48, 384), b(2, 48, 1536), b(2, 192, 384)]
    scratch += [f(4, 48, 384), f(48, 384), f(48, 1536), f(192, 384)]
    scratch += [
        b(2, 4, 128, 768), b(2, 512, 384), b(2, 512, 256), b(6, 512, 512), f(512, 512),
        b(2, 4, 128, 192), b(4, 2, 128, 192), f(256, 768), f(256, 768), f(256, 1), b(256, 768), b(768, 256),
        b(256, 3072), b(256, 3072), b(256, 768), b(256, 768), b(2, 4, 128, 192), b(4, 2, 128, 192),
        b(2, 512, 384), b(2, 512, 256), b(2, 2, 128, 768), b(2, 128, 768),
    ]
    n = 300
    scratch += [pltpu.SemaphoreType.DMA((n,)), pltpu.SemaphoreType.DMA((n,)), pltpu.SemaphoreType.DMA((16,))]
    return pl.pallas_call(
        layer_kernel,
        out_shape=[
            S((2, 128, 768), BF), S((2, 128, 768), F32),
            S((2, 24, 384), F32), S((2, 4, 24, 384), F32), S((2, 24, 1536), F32), S((2, 96, 384), F32), S((16, 768), F32),
        ],
        in_specs=[M, V, V, V, A, A, A, V, V],
        out_specs=[V] * 7,
        scratch_shapes=scratch,
        compiler_params=pltpu.CompilerParams(collective_id=0, has_side_effects=True, vmem_limit_bytes=63 * 2**20),
        cost_estimate=pl.CostEstimate(flops=13 * 10**9, bytes_accessed=10**7, transcendentals=10**7),
    )(lengths, tokens, cot, w, wout, wexp, wshr, vecs, bias_in)


def adam_kernel(o0, oi, o1, o2, osm, out, tgrad, *refs):
    me = lax.axis_index("fsdp")
    ins, outs, bufs, in_sem, out_sem = refs[0:18], refs[20:38], refs[38:56], refs[58], refs[59]
    loads = [pltpu.make_async_copy(ins[k], bufs[k], in_sem.at[k]) for k in range(18)]
    fetch = [pltpu.make_async_copy(a, refs[56 + k], in_sem.at[18 + k]) for k, a in enumerate((out, tgrad))]
    passed = [pltpu.make_async_copy(refs[56 + k], refs[18 + k], out_sem.at[18 + k]) for k in range(2)]
    order = (3, 2, 0, 1, 4, 5)
    for i in order:
        for j in range(3):
            loads[6 * j + i].start()
    for q in fetch:
        q.start()
    w, m, s = bufs[0:6], bufs[6:12], bufs[12:18]
    stores = []

    def arrived(i):
        for j in range(3):
            loads[6 * j + i].wait()

    def leave(i):
        for j in range(3):
            k = 6 * j + i
            stores.append(pltpu.make_async_copy(bufs[k], outs[k], out_sem.at[k]))
            stores[-1].start()

    rates = (2.0 * D ** (-0.5), 4.0 * D ** (-0.5), 2.0 * D ** (-0.5), 2.0 * FF ** (-0.5), 1.0, 1.0)

    def step(i, cols, gradient):
        new = adam_step(w[i][:, cols], gradient, m[i][:, cols], s[i][:, cols], rates[i])
        for j in range(3):
            bufs[6 * j + i][:, cols] = new[j]

    for i, o, n in ((3, o2, 384), (2, o1, 1536)):
        arrived(i)
        for h in range(2):
            step(i, slice(h * n, h * n + n), o[h])
        leave(i)
    arrived(0)
    for j, (h, lane) in enumerate(((0, 0), (0, 192), (1, 0))):
        g = jnp.concatenate([oi[h, q, :, lane : lane + 192] for q in range(4)], 1)
        step(0, slice(j * 768, j * 768 + 768), g)
    leave(0)
    for a, b in zip(fetch, passed):
        a.wait()
        b.start()
    arrived(1)
    for h in range(2):
        step(1, slice(h * 384, h * 384 + 384), o0[h])
    leave(1)
    heads = [jnp.concatenate([osm[12 + q : 13 + q, n : n + 192] for q in range(4)], 1) for n in (0, 256)]
    rows8 = jnp.concatenate([osm[0:2]] + heads + [osm[4:8]], 0)
    rows8 = pltpu.roll(rows8, ((32 - me) % 32) * 24, 1)[:, 0:128]
    arrived(4)
    step(4, slice(0, 24), rows8[:, 0:24])
    leave(4)
    pick = lax.broadcasted_iota(jnp.int32, (4, 1), 0) == me // 8
    row = jnp.sum(jnp.where(pick, osm[8:12], 0.0), 0, keepdims=True)
    row = pltpu.roll(jnp.broadcast_to(row, (8, 768)), ((8 - me % 8) % 8) * 96, 1)
    arrived(5)
    step(5, slice(0, 96), row[0:1, 0:96])
    leave(5)
    for q in passed + stores:
        q.wait()


def adam(grads, out, tgrad, weights, moments, squares):
    args = weights + moments + squares
    V = pl.BlockSpec(memory_space=pltpu.VMEM)
    B = pl.BlockSpec(memory_space=pltpu.HBM)
    n = len(args)
    return pl.pallas_call(
        adam_kernel,
        out_shape=[jax.ShapeDtypeStruct(a.shape, a.dtype) for a in [out, tgrad] + args],
        in_specs=[V] * 5 + [B] * (2 + n),
        out_specs=[B] * (2 + n),
        scratch_shapes=[pltpu.VMEM(a.shape, a.dtype) for a in args + [out, tgrad]] + [pltpu.SemaphoreType.DMA((20,))] * 2,
        compiler_params=pltpu.CompilerParams(vmem_limit_bytes=63 * 2**20),
    )(*grads, out, tgrad, *args)


def body(tokens, cotangent, lengths, input_weight, output_weight, expand_weight, shrink_weight, vectors, expand_bias, *state):
    out, tokens_gradient, o0, oi, o1, o2, os_ = layer(
        lengths, tokens, cotangent, input_weight, output_weight, expand_weight, shrink_weight, vectors.T, expand_bias.reshape(1, 96)
    )
    flat = lambda t: list(t[:4]) + [t[4].T, t[5].reshape(1, 96)]
    weights = (input_weight, output_weight, expand_weight, shrink_weight, vectors, expand_bias)
    new = adam([o0, oi, o1, o2, os_], out, tokens_gradient, flat(weights), flat(state[:6]), flat(state[6:]))
    fix = {4: lambda a: a.T, 5: lambda a: a.reshape(96)}
    return tuple(new[:2]) + tuple(fix.get(i % 6, lambda a: a)(a) for i, a in enumerate(new[2:]))


def solution(mesh):
    in_specs = (
        P("fsdp", "ctx", None),
        P("fsdp", "ctx", None),
        P("fsdp", None),
        P("fsdp", None),
        P("fsdp", None),
        P("fsdp", None),
        P("fsdp", None),
        P("fsdp", None),
        P("fsdp"),
        P("fsdp", None),
        P("fsdp", None),
        P("fsdp", None),
        P("fsdp", None),
        P("fsdp", None),
        P("fsdp"),
        P("fsdp", None),
        P("fsdp", None),
        P("fsdp", None),
        P("fsdp", None),
        P("fsdp", None),
        P("fsdp"),
    )
    out_specs = (
        P("fsdp", "ctx", None),
        P("fsdp", "ctx", None),
        P("fsdp", None),
        P("fsdp", None),
        P("fsdp", None),
        P("fsdp", None),
        P("fsdp", None),
        P("fsdp"),
        P("fsdp", None),
        P("fsdp", None),
        P("fsdp", None),
        P("fsdp", None),
        P("fsdp", None),
        P("fsdp"),
        P("fsdp", None),
        P("fsdp", None),
        P("fsdp", None),
        P("fsdp", None),
        P("fsdp", None),
        P("fsdp"),
    )
    return jax.shard_map(body, mesh=mesh, in_specs=in_specs, out_specs=out_specs, check_vma=False)
```

```python
import jax, jax.numpy as jnp
from jax import lax
from jax.experimental import pallas as pl
from jax.experimental.pallas import tpu as pltpu
from jax.sharding import PartitionSpec as P

MESH = pl.DeviceIdType.MESH
BF = jnp.bfloat16
F32 = jnp.float32


def flip1(v):
    return v + 1 - 2 * (v % 2)


class Links:
    def __init__(self, send_sems, recv_sems):
        self.send_sems, self.recv_sems, self.used = send_sems, recv_sems, 0
        me = lax.axis_index("fsdp")
        self.z = lax.axis_index("ctx")
        self.core = me % 2
        self.chip = me // 2
        self.x, self.y = self.chip // 4, self.chip % 4
        self.sib = {"fsdp": me + 1 - 2 * self.core}
        self.pending = []

    def at(self, axis, kind):
        v = {"x": self.x, "y": self.y, "z": self.z}[axis]
        return flip1(v) if kind == 1 else 3 - v

    def dev(self, axis, kind):
        if axis == "z":
            return {"ctx": self.at("z", kind)}
        x = self.at("x", kind) if axis == "x" else self.x
        y = self.at("y", kind) if axis == "y" else self.y
        return {"fsdp": (x * 4 + y) * 2 + self.core}

    def peers(self, axis):
        v = {"x": self.x, "y": self.y, "z": self.z}[axis]
        others = [flip1(v), 3 - v, (v + 2) % 4]
        if axis == "z":
            return [{"ctx": o} for o in others]
        if axis == "x":
            return [{"fsdp": (o * 4 + self.y) * 2 + self.core} for o in others]
        return [{"fsdp": (self.x * 4 + o) * 2 + self.core} for o in others]

    def send(self, src, dst, device):
        i = self.used
        self.used += 1
        copy = pltpu.make_async_remote_copy(
            src_ref=src, dst_ref=dst, send_sem=self.send_sems.at[i],
            recv_sem=self.recv_sems.at[i], device_id=device, device_id_type=MESH,
        )
        copy.start()
        self.pending.append(copy)
        return copy

    def barrier(self, devices):
        sem = pltpu.get_barrier_semaphore()
        for d in devices:
            pl.semaphore_signal(sem, inc=1, device_id=d, device_id_type=MESH)
        pl.semaphore_wait(sem, len(devices))

    def sent(self, copy):
        copy.wait_send()
        self.pending = [q for q in self.pending if q is not copy]

    def drain(self):
        for c in self.pending:
            c.wait_send()
        self.pending = []


ORDERS = (
    (("y", 1), ("y", 3), ("x", 1), ("x", 3)),
    (("y", 3), ("y", 1), ("x", 3), ("x", 1)),
    (("x", 1), ("x", 3), ("y", 1), ("y", 3)),
    (("x", 3), ("x", 1), ("y", 3), ("y", 1)),
)


def held(v, kind, count):
    if count == 0:
        return [(v, 1)]
    if count == 2:
        return [(0, 4)]
    if kind == 1:
        return [(v - v % 2, 2)]
    return [(v, 1), (3 - v, 1)]


def regions(links, flavor, step, coords):
    order = ORDERS[flavor]
    first, second = order[0][0], order[2][0]
    a = held(coords[first], order[0][1], min(step, 2))
    b = held(coords[second], order[2][1], max(step - 2, 0))
    out = []
    for i, (sa, na) in enumerate(a):
        for j, (sb, nb) in enumerate(b):
            sel = {first: pl.ds(sa, na), second: pl.ds(sb, nb)}
            out.append((sel["x"], sel["y"], i, j, {first: na, second: nb}))
    return out


def gather_step(links, pieces, step):
    copies = []
    for flavor, view in pieces:
        axis, kind = ORDERS[flavor][step]
        device = links.dev(axis, kind)
        for xs, ys, *_ in regions(links, flavor, step, {"x": links.x, "y": links.y}):
            copies.append(links.send(view(xs, ys), view(xs, ys), device))
    return copies


def pair_of(v, kind):
    if kind == 1:
        return [v - v % 2, v - v % 2 + 1]
    return [v, 3 - v]


class Scatter:
    def __init__(self, links, pieces, bufs):
        self.links, self.pieces, self.bufs = links, pieces, bufs

    def _sel(self, flavor, a, b):
        first = ORDERS[flavor][0][0]
        return (a, b) if first == "x" else (b, a)

    def start(self, step):
        L = self.links
        self.copies = []
        for flavor, acc, sub in self.pieces:
            order = ORDERS[flavor]
            axis, kind = order[3 - step]
            first, second = order[0][0], order[2][0]
            va, vb = {"x": L.x, "y": L.y}[first], {"x": L.x, "y": L.y}[second]
            p = L.at(axis, kind)
            dev = L.dev(axis, kind)
            if step == 0:
                for j, b in enumerate(pair_of(p, order[2][1])):
                    self.copies.append(L.send(acc(*self._sel(flavor, pl.ds(0, 4), b)), sub(self.bufs[0].at[j]), dev))
            elif step == 1:
                self.copies.append(L.send(acc(*self._sel(flavor, pl.ds(0, 4), p)), sub(self.bufs[1]), dev))
            elif step == 2:
                for j, a in enumerate(pair_of(p, order[0][1])):
                    self.copies.append(L.send(acc(*self._sel(flavor, a, vb)), sub(self.bufs[2].at[j]), dev))
            else:
                self.copies.append(L.send(acc(*self._sel(flavor, p, vb)), sub(self.bufs[3]), dev))

    def finish(self, step):
        L = self.links
        for c in self.copies:
            c.wait_recv()

        def add(view, buf):
            view[...] = (view[...].astype(F32) + buf[...].astype(F32)).astype(BF)

        for flavor, acc, sub in self.pieces:
            order = ORDERS[flavor]
            first, second = order[0][0], order[2][0]
            va, vb = {"x": L.x, "y": L.y}[first], {"x": L.x, "y": L.y}[second]
            if step == 0:
                for j, b in enumerate(pair_of(vb, order[2][1])):
                    for a in range(4):
                        add(acc(*self._sel(flavor, a, b)), sub(self.bufs[0].at[j, a]))
            elif step == 1:
                for a in range(4):
                    add(acc(*self._sel(flavor, a, vb)), sub(self.bufs[1].at[a]))
            elif step == 2:
                for j, a in enumerate(pair_of(va, order[0][1])):
                    add(acc(*self._sel(flavor, a, vb)), sub(self.bufs[2].at[j]))
            else:
                add(acc(*self._sel(flavor, va, vb)), sub(self.bufs[3]))


def lanes(n, size):
    return lambda ref: ref.at[..., pl.ds(n, size)]


def rows(n, size):
    return lambda ref: ref.at[..., pl.ds(n, size), :]


PIECES = (
    tuple((f, lanes(f * 128, 128)) for f in range(3)) + tuple((3 - f, lanes(384 + f * 128, 128)) for f in range(3)),
    tuple((f, lanes(f * 384, 384)) for f in range(4)),
    tuple((f, rows(f * 48, 48)) for f in range(4)),
)


D = 768
H = 12
HD = 64
FF = 3072
STEP = 10


norm_eps = 1e-05
beta_first = 0.9
beta_second = 0.999
adam_eps = 1e-08
decay_rate = 0.01


def adam_step(weight, gradient, moment, square, rate):
    moment_new = beta_first * moment + (1.0 - beta_first) * gradient
    square_new = beta_second * square + (1.0 - beta_second) * gradient * gradient
    corrected = moment_new / (1.0 - beta_first**STEP)
    spread = jnp.sqrt(square_new / (1.0 - beta_second**STEP)) + adam_eps
    return (weight - rate * (corrected / spread + decay_rate * weight), moment_new, square_new)


NN = ((1,), (0,))
NT = ((1,), (1,))
TN = ((0,), (0,))


def dot(a, b, dims):
    return lax.dot_general(a, b, (dims, ((), ())), preferred_element_type=F32)


def norm_stats(v):
    center = v - jnp.mean(v, -1, keepdims=True)
    r = lax.rsqrt(jnp.mean(center * center, -1, keepdims=True) + norm_eps)
    return center * r, r


def norm_back(z, xhat, r, g):
    zg = z * g
    return r * (zg - jnp.mean(zg, -1, keepdims=True) - xhat * jnp.mean(zg * xhat, -1, keepdims=True))


def colsum(v):
    return jnp.sum(v, 0, keepdims=True)


SHAPES = ((48, 768), (48, 1536), (192, 384))


def layer_kernel(
    lengths, tok, cot, win_all, wout, wexp, wshr, vecs, bias_in,
    out, tgrad, o0, oi, o1, o2, osm,
    win, f0a, f0b, f1, f2, sbuf, gbuf,
    G0, G1, G2, A0, A1, A2, S0, S1, S2,
    R00, R01, R02, R03, R10, R11, R12, R13, R20, R21, R22, R23,
    zi, z0, z1, z2, fi, f0f, f1f, f2f,
    X, QK, V, P, MB, CS, CT, after, xh2, r2, second, sect, hidden, slope, up, ab, CBS, CB, PQK, PV, N1, N2,
    ss, rs, ls,
):
    L = Links(ss, rs)
    c, z, x, y = L.core, L.z, L.x, L.y
    me = {"x": x, "y": y}
    zf, zt, zo = L.at("z", 1), L.at("z", 3), (z + 2) % 4
    zpeers = (zf, zt, zo)
    G, A, S = [G0, G1, G2], [A0, A1, A2], [S0, S1, S2]

    def wait(copies):
        for q in copies:
            q.wait_recv()

    local = [0]

    def move(src, dst):
        cp = pltpu.make_async_copy(src, dst, ls.at[local[0]])
        local[0] += 1
        cp.start()
        return cp

    class Sum:
        def __init__(self, buf):
            self.buf = buf

        def start(self, axis):
            base = 1 + 4 * "cyxz".index(axis)
            v, to = {"c": (c, [L.sib]), "x": (x, L.peers("x")), "y": (y, L.peers("y")), "z": (z, L.peers("z"))}[axis]
            self.buf[base + v] = self.buf[0]
            self.slots = [base + i for i in range(len(to) + 1)]
            self.copies = [L.send(self.buf.at[base + v], self.buf.at[base + v], d) for d in to]

        def finish(self):
            wait(self.copies)
            total = self.buf[self.slots[0]]
            for i in self.slots[1:]:
                total = total + self.buf[i]
            self.buf[0] = total

    small = Sum(sbuf)
    me_all = lax.axis_index("fsdp")
    tiled = vecs[...]
    for _ in range(5):
        tiled = jnp.concatenate([tiled, tiled], 1)
    lane = lax.broadcasted_iota(jnp.int32, (1, 768), 1)
    first = me_all * 24
    sbuf[0] = jnp.zeros((16, 768), F32)
    sbuf[0, 0:8] = jnp.where((lane >= first) & (lane < first + 24), tiled, 0.0)
    near = (lane + z * 192 >= first) & (lane + z * 192 < first + 24) & (lane < 192)
    sbuf[0, 12:14] = jnp.where(near, tiled[2:4], 0.0)
    tiled = jnp.broadcast_to(bias_in[...], (4, 96))
    for _ in range(3):
        tiled = jnp.concatenate([tiled, tiled], 1)
    first = (me_all % 8) * 96
    here = (lax.broadcasted_iota(jnp.int32, (4, 1), 0) == me_all // 8) & (lane >= first) & (lane < first + 96)
    sbuf[0, 8:12] = jnp.where(here, tiled, 0.0)
    sbuf[0] = sbuf[0].astype(BF).astype(F32)
    for j in range(3):
        cut = [win_all[:, j * 768 + q * 192 : j * 768 + q * 192 + 192] for q in range(4)]
        win[:, j * 192 : j * 192 + 192] = jnp.where(z == 0, cut[0], jnp.where(z == 1, cut[1], jnp.where(z == 2, cut[2], cut[3])))
    win[:, 576:768] = jnp.zeros((24, 192), F32)
    L.barrier([L.sib] + L.peers("x") + L.peers("y") + L.peers("z"))
    small.start("c")

    def halves(src, n, dst, nr):
        other, mine = pl.multiple_of((1 - c) * n, 128), pl.multiple_of(c * n, 128)
        r = pl.ds(pl.multiple_of(nr * c, 8), nr)
        return L.send(src.at[:, pl.ds(other, n)], dst.at[r], L.sib), move(src.at[:, pl.ds(mine, n)], dst.at[r])

    pairs = [halves(win, 384, f0a, 24), halves(wout, 384, f0b, 24)]
    xl = move(tok, X.at[:, z])
    tz = []
    for p in range(2):
        for h, k in enumerate((1, 3)):
            r = pl.ds(h * 64, 64)
            tz.append(L.send(tok.at[p, r], X.at[p, z, r], L.dev("z", k)))
    pairs += [halves(wexp, 1536, f1, 24), halves(wshr, 384, f2, 96)]

    views = []
    for g in range(3):
        views.append([(f, (lambda sub, g: lambda xs, ys: sub(G[g].at[c, xs, ys]))(sub, g)) for f, sub in PIECES[g]])
    flight = {}

    def start(g, s):
        flight[g] = gather_step(L, views[g], s)

    def advance(g, s):
        wait(flight[g])
        start(g, s)

    def to_sibling(g, arrived):
        res = []
        for f, view in views[g]:
            axis, kind = ORDERS[f][3]
            o = dict(me)
            if arrived:
                o[axis] = L.at(axis, kind)
            for xs, ys, *_ in regions(L, f, 3, o):
                res.append(L.send(view(xs, ys), view(xs, ys), L.sib))
        return res

    for cp, lc in pairs[:2]:
        cp.wait_recv()
        lc.wait()
    G0[c, x, y, :, 0:384] = f0a[...].astype(BF)
    G0[c, x, y, :, 384:768] = f0b[...].astype(BF)
    start(0, 0)
    small.finish()
    small.start("y")
    for g, f in ((1, f1), (2, f2)):
        cp, lc = pairs[g + 1]
        cp.wait_recv()
        lc.wait()
        G[g][c, x, y] = f[...].astype(BF)
        start(g, 0)
    advance(0, 1)
    small.finish()
    small.start("x")
    xl.wait()
    tz2 = []
    for p in range(2):
        for h, (k1, k2) in enumerate(((1, 3), (3, 1))):
            r = pl.ds(h * 64, 64)
            tz[2 * p + h].wait_recv()
            q = L.at("z", k1)
            tz2.append([L.send(X.at[p, b, r], X.at[p, b, r], L.dev("z", k2)) for b in (z, q)])
    advance(0, 2)
    advance(1, 1)
    advance(2, 1)
    advance(0, 3)
    sib = {0: to_sibling(0, False)}

    seqs = lengths.shape[1]

    def segment(p, shape, dim):
        pos = lax.broadcasted_iota(jnp.int32, shape, dim)
        end = lengths[p, 0]
        seg = (pos >= end).astype(jnp.int32)
        for i in range(1, seqs):
            end = end + lengths[p, i]
            seg = seg + (pos >= end).astype(jnp.int32)
        return seg

    def fill_mask(p):
        ok = segment(p, (512, 1), 0) == segment(p, (1, 512), 1)
        ok = ok & (lax.broadcasted_iota(jnp.int32, (512, 512), 1) <= lax.broadcasted_iota(jnp.int32, (512, 512), 0))
        MB[...] = jnp.where(ok, 0.0, -1e30)

    def live_rows(p):
        pos = lax.broadcasted_iota(jnp.int32, (128, 1), 0) + z * 128
        total = lengths[p, 0]
        for i in range(1, seqs):
            total = total + lengths[p, i]
        return (pos < total).astype(F32)

    small.finish()
    g1, b1 = sbuf[0, 0:1], sbuf[0, 1:2]

    def ready(p):
        for q in tz2[2 * p] + tz2[2 * p + 1]:
            q.wait_recv()
            L.sent(q)

    def project(p):
        for b in range(4):
            xhat, _ = norm_stats(X[p, b].astype(F32))
            X[p, b] = (xhat * g1 + b1).astype(BF)

    def qkv(p):
        n = X[p].reshape(512, 768)
        qk = dot(n, G0[0, :, :, :, 0:384].reshape(768, 384), NN)
        q = (qk[:, 0:192] + sbuf[0, 12:13, 0:192]) * 0.125
        QK[p] = jnp.concatenate([q, qk[:, 192:384]], 1).astype(BF)
        V[p] = (dot(n, G0[1, :, :, :, 0:256].reshape(768, 256), NN) + sbuf[0, 13:14, 0:256]).astype(BF)

    def attend(p):
        parts = [[], []]
        for h in range(3):
            q = QK[p, :, h * 64 : h * 64 + 64]
            k = QK[p, :, 192 + h * 64 : 256 + h * 64]
            v = V[p, :, h * 64 : h * 64 + 64]
            for i in range(2):
                r, n = i * 256, (i + 1) * 256
                s = dot(q[r : r + 256], k[:n], NT) + MB[r : r + 256, 0:n]
                e = jnp.exp(s - jnp.max(s, -1, keepdims=True))
                pr = (e * (1.0 / jnp.sum(e, -1, keepdims=True))).astype(BF)
                P[p * 3 + h, r : r + 256, 0:n] = pr
                parts[i].append(dot(pr, v[:n], NN))
        for i in range(2):
            ctx = jnp.concatenate(parts[i], 1).astype(BF)
            CS[p, 2 * i : 2 * i + 2] = ctx.reshape(2, 128, 192)

    def to_heads_owner(p, src, dst):
        res = [L.send(src.at[p, q], dst.at[z, p], {"ctx": q}) for q in zpeers]
        return res

    fill_mask(0)
    advance(1, 2)
    advance(2, 2)
    wait(flight[0])
    sib[0] += to_sibling(0, True)
    ready(0)
    project(0)
    wait(sib[0])
    qkv(0)
    advance(1, 3)
    sib[1] = to_sibling(1, False)
    attend(0)
    ctx_moves = to_heads_owner(0, CS, CT)
    own = [move(CS.at[0, z], CT.at[z, 0])]
    advance(2, 3)
    sib[2] = to_sibling(2, False)
    ready(1)
    project(1)
    fill_mask(1)
    qkv(1)
    attend(1)
    ctx_moves += to_heads_owner(1, CS, CT)
    own.append(move(CS.at[1, z], CT.at[z, 1]))
    wait(flight[1])
    sib[1] += to_sibling(1, True)
    for q in own:
        q.wait()
    wait(ctx_moves)

    bo, g2, b2, bd = sbuf[0, 4:5], sbuf[0, 5:6], sbuf[0, 6:7], sbuf[0, 7:8]
    for h in range(2):
        acc = sbuf[0, 4:5, h * 384 : h * 384 + 384] + tok[:, :, h * 384 : h * 384 + 384].astype(F32).reshape(256, 384)
        for q in range(4):
            acc = acc + dot(CT[q].reshape(256, 192), G0[h, q, :, :, 384:768].reshape(192, 384), NN)
        after[:, h * 384 : h * 384 + 384] = acc
    xhat, r = norm_stats(after[...])
    xh2[...] = xhat
    r2[...] = r
    sec = (xhat * g2 + b2).astype(BF)
    second[...] = sec
    sect[...] = sec.T
    live = [live_rows(p) for p in range(2)]
    for p in range(2):
        up[p * 128 : p * 128 + 128] = cot[p] * live[p].astype(BF)

    wait(sib[1])
    for t in range(4):
        lane = (t % 2) * 768
        e = dot(second[...], G1[t // 2, :, :, :, lane : lane + 768].reshape(768, 768), NN) + sbuf[0, 8 + t : 9 + t]
        cdf = 0.5 * (1.0 + lax.erf(e * (2.0 ** -0.5)))
        hidden[:, t * 768 : t * 768 + 768] = (e * cdf).astype(BF)
        slope[:, t * 768 : t * 768 + 768] = (cdf + e * (jnp.exp(-0.5 * e * e) * 0.3989422804014327)).astype(BF)
    for t in range(4):
        for h in range(2):
            d = dot(hidden[:, t * 768 : t * 768 + 768], up[:, h * 384 : h * 384 + 384], TN)
            A2[h, t] = d.astype(BF).reshape(4, 192, 384)

    def pieces_of(i):
        return [(f, (lambda sub: lambda xs, ys: sub(A[i].at[c, xs, ys]))(sub), sub) for f, sub in PIECES[i]]

    bufs = [[R00, R01, R02, R03], [R10, R11, R12, R13], [R20, R21, R22, R23]]
    sc = {1: Scatter(L, pieces_of(1), bufs[1]), 2: Scatter(L, pieces_of(2), bufs[2])}
    sc["in"] = Scatter(L, pieces_of(0)[:3], bufs[0])
    sc["out"] = Scatter(L, pieces_of(0)[3:], bufs[0])
    pair = {}
    split = {"in": lanes(0, 384), "out": lanes(384, 384)}

    def pair_start(i):
        if i in split:
            pair[i] = L.send(split[i](A0.at[1 - c]), split[i](S0), L.sib)
        else:
            pair[i] = L.send(A[i].at[1 - c], S[i], L.sib)

    def pair_finish(i):
        pair[i].wait_recv()

        @pl.loop(0, 4)
        def _(k):
            if i in split:
                a, b = split[i](A0.at[c, k]), split[i](S0.at[k])
            else:
                a, b = A[i].at[c, k], S[i].at[k]
            a[...] = (a[...].astype(F32) + b[...].astype(F32)).astype(BF)

        sc[i].start(0)

    def turn(i, s):
        sc[i].finish(s)
        if s < 3:
            sc[i].start(s + 1)

    pair_start(2)

    wait(flight[2])
    sib[2] += to_sibling(2, True)
    pair_finish(2)
    wait(sib[2])

    for h in range(2):
        w = after[:, h * 384 : h * 384 + 384] + bd[:, h * 384 : h * 384 + 384]
        for t in range(4):
            w = w + dot(hidden[:, t * 768 : t * 768 + 768], G2[h, t].reshape(768, 384), NN)
        for p in range(2):
            out[p, :, h * 384 : h * 384 + 384] = (w[p * 128 : p * 128 + 128] * live[p]).astype(BF)

    resid = after
    gsum = Sum(gbuf)
    for t in range(4):
        lane = (t % 2) * 768
        cols = pl.ds(t * 768, 768)
        hb = dot(up[:, 0:384], G2[0, t].reshape(768, 384), NT) + dot(up[:, 384:768], G2[1, t].reshape(768, 384), NT)
        eb = (hb * slope[:, cols].astype(F32)).astype(BF)
        hidden[:, cols] = eb
        gbuf[0, 8 + t : 9 + t] = colsum(eb.astype(F32))
        part = dot(eb, G1[t // 2, :, :, :, lane : lane + 768].reshape(768, 768), NT)
        if t == 0:
            resid[...] = part
        else:
            resid[...] += part
        for q in range(4):
            d = dot(sect[q * 192 : q * 192 + 192], eb, NN).astype(BF)
            A1[t // 2, q, :, :, lane : lane + 768] = d.reshape(4, 48, 768)
    pair_start(1)
    turn(2, 0)
    sb = resid[...]
    gbuf[0, 5:6] = colsum(sb * xh2[...])
    gbuf[0, 6:7] = colsum(sb)
    up32 = up[...].astype(F32)
    gbuf[0, 7:8] = colsum(up32)
    res = up32 + norm_back(sb, xh2[...], r2[...], g2)
    resid[...] = res
    ab[...] = res.astype(BF)
    gbuf[0, 4:5] = colsum(ab[...].astype(F32))

    for q in range(4):
        d = dot(ab[:, 0:384], G0[0, q, :, :, 384:768].reshape(192, 384), NT)
        d = d + dot(ab[:, 384:768], G0[1, q, :, :, 384:768].reshape(192, 384), NT)
        CBS[:, q] = d.astype(BF).reshape(2, 128, 192)
    back_moves = [to_heads_owner(p, CBS, CB) for p in range(2)]
    own = [move(CBS.at[p, z], CB.at[z, p]) for p in range(2)]
    for q in range(4):
        d = dot(CT[q].reshape(256, 192), ab[...], TN).astype(BF)
        for h in range(2):
            A0[h, q, :, :, 384:768] = d[:, h * 384 : h * 384 + 384].reshape(4, 48, 384)
    pair_start("out")
    pair_finish(1)
    turn(2, 1)
    pair_finish("out")

    def attend_back(p):
        co = CB[:, p].reshape(512, 192)
        dqs, dks, dvs = [[], []], [], []
        for h in range(3):
            do = co[:, h * 64 : h * 64 + 64]
            q = QK[p, :, h * 64 : h * 64 + 64]
            k = QK[p, :, 192 + h * 64 : 256 + h * 64]
            v = V[p, :, h * 64 : h * 64 + 64]
            dk, dv = [], []
            for i in range(2):
                r, n = i * 256, (i + 1) * 256
                pr = P[p * 3 + h, r : r + 256, 0:n]
                p32 = pr.astype(F32)
                dp = dot(do[r : r + 256], v[:n], NT)
                ds = (p32 * (dp - jnp.sum(p32 * dp, -1, keepdims=True))).astype(BF)
                dqs[i].append(dot(ds, k[:n], NN) * 0.125)
                dk.append(dot(ds, q[r : r + 256], TN))
                dv.append(dot(pr, do[r : r + 256], TN))
            dks.append([dk[0] + dk[1][:256], dk[1][256:]])
            dvs.append([dv[0] + dv[1][:256], dv[1][256:]])
        for i in range(2):
            r = i * 256
            PQK[p, r : r + 256] = jnp.concatenate(dqs[i] + [d[i] for d in dks], 1).astype(BF)
            PV[p, r : r + 256] = jnp.concatenate([d[i] for d in dvs] + [jnp.zeros((256, 64), F32)], 1).astype(BF)

    def NB(p, b):
        lane = b * 768 if isinstance(b, int) else pl.multiple_of(b * 768, 128)
        return hidden.at[pl.ds(p * 128, 128), pl.ds(lane, 768)]

    nb_moves = [None, None]
    kinds = ((1, 3), (3, 1))

    def inner_back(p):
        n = dot(PQK[p], G0[0, :, :, :, 0:384].reshape(768, 384), NT)
        n = n + dot(PV[p], G0[1, :, :, :, 0:256].reshape(768, 256), NT)
        for b in range(4):
            NB(p, b)[...] = n[b * 128 : b * 128 + 128].astype(BF)
        k1, k2 = kinds[p]
        q = L.at("z", k1)
        nb_moves[p] = [L.send(NB(p, b), N1.at[p, j], L.dev("z", k1)) for j, b in enumerate((q, zo if k2 != k1 else q))]

    for p in range(2):
        own[p].wait()
        wait(back_moves[p])
        attend_back(p)
        inner_back(p)
        if p == 0:
            turn(2, 2)
            turn(1, 0)
    for q in range(2):
        xs, n = slice(2 * q, 2 * q + 2), X[:, :, :, q * 384 : q * 384 + 384].reshape(1024, 384)
        A0[0, xs, :, :, 0:384] = dot(n, PQK[...].reshape(1024, 384), TN).astype(BF).reshape(2, 4, 48, 384)
        A0[1, xs, :, :, 0:256] = dot(n, PV[...].reshape(1024, 256), TN).astype(BF).reshape(2, 4, 48, 256)
    A0[1, :, :, :, 256:384] = jnp.zeros((4, 4, 48, 128), BF)
    pair_start("in")
    gbuf[0, 0:4] = jnp.zeros((4, 768), F32)
    gbuf[0, 12:16] = jnp.zeros((4, 768), F32)
    mine = lax.broadcasted_iota(jnp.int32, (4, 1), 0) == z
    sq = colsum(PQK[...].reshape(1024, 384)[:, 0:256].astype(F32))
    sv = colsum(PV[...].reshape(1024, 256).astype(F32))
    gbuf[0, 12:16, 0:256] = jnp.where(mine, sq, 0.0)
    gbuf[0, 12:16, 256:512] = jnp.where(mine, sv, 0.0)
    zb = [z0, z1, z2]
    W = [A0.at[c, x, y, :, pl.ds(384, 384)], A1.at[c, x, y], A2.at[c, x, y]]
    CUT = [(lanes(0, 128), lanes(128, 256)), (lanes(0, 768), lanes(768, 768)), (rows(0, 96), rows(96, 96))]
    zc, zc2 = {}, {}

    def z_start(i):
        zc[i] = [L.send(CUT[i][h](W[i]), CUT[i][h](zb[i].at[0]), L.dev("z", k)) for h, k in enumerate((1, 3))]

    def z_turn(i):
        zc2[i] = []
        for h, k in enumerate((3, 1)):
            q = zc[i][h]
            q.wait_recv()
            L.sent(q)
            v = CUT[i][h](W[i])
            v[...] = (v[...].astype(F32) + CUT[i][h](zb[i].at[0])[...].astype(F32)).astype(BF)
            zc2[i].append(L.send(v, CUT[i][h](zb[i].at[1]), L.dev("z", k)))

    fin, loc = [], []

    def hand(src, dst, nr):
        oth, ours = pl.multiple_of((1 - c) * nr, 8), pl.multiple_of(c * nr, 8)
        fin.append(L.send(src.at[..., pl.ds(oth, nr), :], dst.at[c], L.sib))
        loc.append(move(src.at[..., pl.ds(ours, nr), :], dst.at[c]))

    def z_finish(i, f, o, nr):
        for h in range(2):
            zc2[i][h].wait_recv()
            CUT[i][h](f)[...] = CUT[i][h](W[i])[...].astype(F32) + CUT[i][h](zb[i].at[1])[...].astype(F32)
        hand(f, o, nr)

    turn(2, 3)
    z_start(2)
    turn("out", 0)
    turn(1, 1)
    pair_finish("in")
    turn("out", 1)

    second_moves = []
    for p in range(2):
        k1, k2 = kinds[p]
        wait(nb_moves[p])
        q = L.at("z", k2)
        NB(p, q)[...] = (NB(p, q)[...].astype(F32) + N1[p, 1].astype(F32)).astype(BF)
        second_moves.append(L.send(NB(p, q), N2.at[p], L.dev("z", k2)))
    turn(1, 2)
    turn("out", 2)
    turn("in", 0)
    z_turn(2)
    turn(1, 3)
    z_start(1)
    turn("out", 3)
    z_start(0)
    turn("in", 1)
    z_finish(2, f2f, o2, 96)
    turn("in", 2)
    z_turn(1)
    z_turn(0)
    for p in range(2):
        second_moves[p].wait_recv()
        rows_p = slice(p * 128, p * 128 + 128)
        nb = NB(p, z)[...].astype(F32) + N1[p, 0].astype(F32) + N2[p].astype(F32)
        xhat, r = norm_stats(tok[p].astype(F32))
        tgrad[p] = resid[rows_p] + norm_back(nb, xhat, r, g1)
        gbuf[0, 0:1] += colsum(nb * xhat)
        gbuf[0, 1:2] += colsum(nb)
    gsum.start("c")
    turn("in", 3)
    zi[z] = A0[c, x, y, :, 0:384]
    zic = [L.send(zi.at[z], zi.at[z], d) for d in L.peers("z")]
    gsum.finish()
    gsum.start("z")
    z_finish(1, f1f, o1, 24)
    z_finish(0, f0f, o0, 24)
    wait(zic)
    fi[...] = zi[...].astype(F32)
    hand(fi, oi, 24)
    gsum.finish()
    gsum.start("y")
    gsum.finish()
    gsum.start("x")
    wait(fin)
    for q in loc:
        q.wait()
    gsum.finish()
    osm[...] = gbuf[0]
    L.drain()


def layer(lengths, tokens, cot, w, wout, wexp, wshr, vecs, bias_in):
    V = pl.BlockSpec(memory_space=pltpu.VMEM)
    A = pl.BlockSpec(memory_space=pltpu.HBM)
    M = pl.BlockSpec(memory_space=pltpu.SMEM)
    S = jax.ShapeDtypeStruct
    b = lambda *s: pltpu.VMEM(s, BF)
    f = lambda *s: pltpu.VMEM(s, F32)
    scratch = [f(24, 768), f(48, 384), f(48, 384), f(48, 1536), f(192, 384), f(13, 16, 768), f(17, 16, 768)]
    scratch += [b(2, 4, 4, *s) for s in SHAPES] * 2 + [b(4, 4, *s) for s in SHAPES]
    for s in SHAPES:
        scratch += [b(2, 4, *s), b(4, *s), b(2, *s), b(*s)]
    scratch += [b(4, 48, 384), b(2, 48, 384), b(2, 48, 1536), b(2, 192, 384)]
    scratch += [f(4, 48, 384), f(48, 384), f(48, 1536), f(192, 384)]
    scratch += [
        b(2, 4, 128, 768), b(2, 512, 384), b(2, 512, 256), b(6, 512, 512), f(512, 512),
        b(2, 4, 128, 192), b(4, 2, 128, 192), f(256, 768), f(256, 768), f(256, 1), b(256, 768), b(768, 256),
        b(256, 3072), b(256, 3072), b(256, 768), b(256, 768), b(2, 4, 128, 192), b(4, 2, 128, 192),
        b(2, 512, 384), b(2, 512, 256), b(2, 2, 128, 768), b(2, 128, 768),
    ]
    n = 300
    scratch += [pltpu.SemaphoreType.DMA((n,)), pltpu.SemaphoreType.DMA((n,)), pltpu.SemaphoreType.DMA((16,))]
    return pl.pallas_call(
        layer_kernel,
        out_shape=[
            S((2, 128, 768), BF), S((2, 128, 768), F32),
            S((2, 24, 384), F32), S((2, 4, 24, 384), F32), S((2, 24, 1536), F32), S((2, 96, 384), F32), S((16, 768), F32),
        ],
        in_specs=[M, V, V, V, A, A, A, V, V],
        out_specs=[V] * 7,
        scratch_shapes=scratch,
        compiler_params=pltpu.CompilerParams(collective_id=0, has_side_effects=True, vmem_limit_bytes=63 * 2**20),
        cost_estimate=pl.CostEstimate(flops=13 * 10**9, bytes_accessed=10**7, transcendentals=10**7),
    )(lengths, tokens, cot, w, wout, wexp, wshr, vecs, bias_in)


def adam_kernel(o0, oi, o1, o2, osm, out, tgrad, *refs):
    me = lax.axis_index("fsdp")
    ins, outs, bufs, in_sem, out_sem = refs[0:18], refs[20:38], refs[38:56], refs[58], refs[59]
    loads = [pltpu.make_async_copy(ins[k], bufs[k], in_sem.at[k]) for k in range(18)]
    fetch = [pltpu.make_async_copy(a, refs[56 + k], in_sem.at[18 + k]) for k, a in enumerate((out, tgrad))]
    passed = [pltpu.make_async_copy(refs[56 + k], refs[18 + k], out_sem.at[18 + k]) for k in range(2)]
    order = (3, 2, 0, 1, 4, 5)
    for i in order:
        for j in range(3):
            loads[6 * j + i].start()
    for q in fetch:
        q.start()
    w, m, s = bufs[0:6], bufs[6:12], bufs[12:18]
    stores = []

    def arrived(i):
        for j in range(3):
            loads[6 * j + i].wait()

    def leave(i):
        for j in range(3):
            k = 6 * j + i
            stores.append(pltpu.make_async_copy(bufs[k], outs[k], out_sem.at[k]))
            stores[-1].start()

    rates = (2.0 * D ** (-0.5), 4.0 * D ** (-0.5), 2.0 * D ** (-0.5), 2.0 * FF ** (-0.5), 1.0, 1.0)

    def step(i, cols, gradient):
        new = adam_step(w[i][:, cols], gradient, m[i][:, cols], s[i][:, cols], rates[i])
        for j in range(3):
            bufs[6 * j + i][:, cols] = new[j]

    for i, o, n in ((3, o2, 384), (2, o1, 1536)):
        arrived(i)
        for h in range(2):
            step(i, slice(h * n, h * n + n), o[h])
        leave(i)
    arrived(0)
    for j, (h, lane) in enumerate(((0, 0), (0, 192), (1, 0))):
        g = jnp.concatenate([oi[h, q, :, lane : lane + 192] for q in range(4)], 1)
        step(0, slice(j * 768, j * 768 + 768), g)
    leave(0)
    for a, b in zip(fetch, passed):
        a.wait()
        b.start()
    arrived(1)
    for h in range(2):
        step(1, slice(h * 384, h * 384 + 384), o0[h])
    leave(1)
    heads = [jnp.concatenate([osm[12 + q : 13 + q, n : n + 192] for q in range(4)], 1) for n in (0, 256)]
    rows8 = jnp.concatenate([osm[0:2]] + heads + [osm[4:8]], 0)
    rows8 = pltpu.roll(rows8, ((32 - me) % 32) * 24, 1)[:, 0:128]
    arrived(4)
    step(4, slice(0, 24), rows8[:, 0:24])
    leave(4)
    pick = lax.broadcasted_iota(jnp.int32, (4, 1), 0) == me // 8
    row = jnp.sum(jnp.where(pick, osm[8:12], 0.0), 0, keepdims=True)
    row = pltpu.roll(jnp.broadcast_to(row, (8, 768)), ((8 - me % 8) % 8) * 96, 1)
    arrived(5)
    step(5, slice(0, 96), row[0:1, 0:96])
    leave(5)
    for q in passed + stores:
        q.wait()


def adam(grads, out, tgrad, weights, moments, squares):
    args = weights + moments + squares
    V = pl.BlockSpec(memory_space=pltpu.VMEM)
    B = pl.BlockSpec(memory_space=pltpu.HBM)
    n = len(args)
    return pl.pallas_call(
        adam_kernel,
        out_shape=[jax.ShapeDtypeStruct(a.shape, a.dtype) for a in [out, tgrad] + args],
        in_specs=[V] * 5 + [B] * (2 + n),
        out_specs=[B] * (2 + n),
        scratch_shapes=[pltpu.VMEM(a.shape, a.dtype) for a in args + [out, tgrad]] + [pltpu.SemaphoreType.DMA((20,))] * 2,
        compiler_params=pltpu.CompilerParams(vmem_limit_bytes=63 * 2**20),
    )(*grads, out, tgrad, *args)


def body(tokens, cotangent, lengths, input_weight, output_weight, expand_weight, shrink_weight, vectors, expand_bias, *state):
    out, tokens_gradient, o0, oi, o1, o2, os_ = layer(
        lengths, tokens, cotangent, input_weight, output_weight, expand_weight, shrink_weight, vectors.T, expand_bias.reshape(1, 96)
    )
    flat = lambda t: list(t[:4]) + [t[4].T, t[5].reshape(1, 96)]
    weights = (input_weight, output_weight, expand_weight, shrink_weight, vectors, expand_bias)
    new = adam([o0, oi, o1, o2, os_], out, tokens_gradient, flat(weights), flat(state[:6]), flat(state[6:]))
    fix = {4: lambda a: a.T, 5: lambda a: a.reshape(96)}
    return tuple(new[:2]) + tuple(fix.get(i % 6, lambda a: a)(a) for i, a in enumerate(new[2:]))


def solution(mesh):
    in_specs = (
        P("fsdp", "ctx", None),
        P("fsdp", "ctx", None),
        P("fsdp", None),
        P("fsdp", None),
        P("fsdp", None),
        P("fsdp", None),
        P("fsdp", None),
        P("fsdp", None),
        P("fsdp"),
        P("fsdp", None),
        P("fsdp", None),
        P("fsdp", None),
        P("fsdp", None),
        P("fsdp", None),
        P("fsdp"),
        P("fsdp", None),
        P("fsdp", None),
        P("fsdp", None),
        P("fsdp", None),
        P("fsdp", None),
        P("fsdp"),
    )
    out_specs = (
        P("fsdp", "ctx", None),
        P("fsdp", "ctx", None),
        P("fsdp", None),
        P("fsdp", None),
        P("fsdp", None),
        P("fsdp", None),
        P("fsdp", None),
        P("fsdp"),
        P("fsdp", None),
        P("fsdp", None),
        P("fsdp", None),
        P("fsdp", None),
        P("fsdp", None),
        P("fsdp"),
        P("fsdp", None),
        P("fsdp", None),
        P("fsdp", None),
        P("fsdp", None),
        P("fsdp", None),
        P("fsdp"),
    )
    return jax.shard_map(body, mesh=mesh, in_specs=in_specs, out_specs=out_specs, check_vma=False)
```
